32 devices in a mesh: groups: 2 (over y), row: 4 (over x, core), col: 4 (over z).
Axes of the slice: x: 2, y: 2, z: 4, core: 2. Of those that a mesh axis runs over, the one named last changes fastest.
Arguments:
- queries: bfloat16 [4096, 512], P(('groups', 'row', 'col')), parts along dimension 0, may hold values from -6 to 6
- keys: bfloat16 [4096, 512], P(('groups', 'col', 'row')), parts along dimension 0, may hold values from -6 to 6
- values: bfloat16 [4096, 512], P(('groups', 'col', 'row')), parts along dimension 0, may hold values from -6 to 6
- outputs: bfloat16 [4096, 512], P(('groups', 'row', 'col')), parts along dimension 0, may hold values from -6 to 6
- out_grad: bfloat16 [4096, 512], P(('groups', 'row', 'col')), parts along dimension 0, may hold values from -192 to 192
- log_norm: float32 [8, 4096], P(None, ('groups', 'row', 'col')), parts along dimension 1, may hold values from 7 to 9
- contacts: int32 [32, 12], P(('groups', 'row')), parts along dimension 0, may hold values from 0 to 15, as said below
Outputs:
- query_grads: bfloat16 [4096, 512], P(('groups', 'row', 'col')), parts along dimension 0
- key_grads: bfloat16 [4096, 512], P(('groups', 'col', 'row')), parts along dimension 0
- value_grads: bfloat16 [4096, 512], P(('groups', 'col', 'row')), parts along dimension 0
The draws below stay inside these ranges and needn't reach their ends.
There are 2 independent parts, one for each index of `groups`. The reference program is written for one: setup_inputs(seed, part) draws one part's arguments, and reference() takes and returns one part's arrays. A program takes and returns all parts, laid end to end along the dimension named above; each array names one. Nothing has to cross between parts.
Inputs may be any that keep to these rules, and one draw needn't show every extreme that they name: `contacts`: each row lists 12 distinct key blocks, among them the row's own index; counting key blocks in aligned groups of 4 consecutive blocks, at most 4 of a row's entries lie in one group, and exactly 4 lie in the group that holds the row's own block.
All inputs are finite; a program needn't handle non-finite values.
Results may differ from the reference program's by a relative error of at most 0.0066.
Values may be sent and summed in bfloat16 or wider, within the bound.
No kernel may reach another device: no remote copies, remote signals or barrier semaphores. Data moves between devices by JAX's collectives and lax.ppermute only.
A program may use at most 128 MiB of HBM per device.

```python
import math
import jax
import jax.numpy as jnp
from jax import lax

D = 512
H = 8
BLOCK = 128
KNB = 12
MOST = 4
TOKENS = 2048
NB = 16
TILES_PER_SET = 4


def draw_contacts(key, part):
    key = jax.random.fold_in(key, 11)
    pick_key = jax.random.fold_in(key, 1)
    place_key = jax.random.fold_in(key, 2)
    order_key = jax.random.fold_in(key, 3)
    group_count = NB // TILES_PER_SET
    spare_count = KNB - MOST
    slot_total = (group_count - 1) * MOST
    row_ids = jnp.arange(NB, dtype=jnp.int32)
    own_group = row_ids // TILES_PER_SET
    own_local = row_ids % TILES_PER_SET
    within_set_positions = jnp.arange(TILES_PER_SET, dtype=jnp.int32)
    group_ids = jnp.arange(group_count, dtype=jnp.int32)
    raw_logits = jax.random.randint(pick_key, (NB, group_count, TILES_PER_SET), 0, 65536, dtype=jnp.int32)
    self_tile_found = (group_ids[None, :, None] == own_group[:, None, None]) & (within_set_positions[None, None, :] == own_local[:, None, None])
    logit_offset = jnp.where(self_tile_found, 65536, 0).astype(jnp.int32)
    sorted_position = (raw_logits + logit_offset) * TILES_PER_SET + within_set_positions[None, None, :]
    top_scores, picked = lax.top_k(sorted_position, MOST)
    blocks = group_ids[None, :, None] * TILES_PER_SET + picked.astype(jnp.int32)
    own_picks = jnp.sum(jnp.where(group_ids[None, :, None] == own_group[:, None, None], blocks, 0), axis=1)
    other_ids = jnp.arange(group_count - 1, dtype=jnp.int32)
    other_groups = other_ids[None, :] + (other_ids[None, :] >= own_group[:, None]).astype(jnp.int32)
    other_index = jnp.broadcast_to(other_groups[:, :, None], (NB, group_count - 1, MOST))
    other_blocks = jnp.take_along_axis(blocks, other_index, axis=1)
    flat_other = other_blocks.reshape(NB, slot_total)
    place_raw = jax.random.randint(place_key, (NB, slot_total), 0, 65536, dtype=jnp.int32)
    place_rank = place_raw * slot_total + jnp.arange(slot_total, dtype=jnp.int32)[None, :]
    ignored, chosen = lax.top_k(place_rank, spare_count)
    far_blocks = jnp.take_along_axis(flat_other, chosen.astype(jnp.int32), axis=1)
    listed = jnp.concatenate([own_picks, far_blocks], axis=1)
    order_raw = jax.random.randint(order_key, (NB, KNB), 0, 65536, dtype=jnp.int32)
    order_rank = order_raw * KNB + jnp.arange(KNB, dtype=jnp.int32)[None, :]
    unused, shuffle = lax.top_k(order_rank, KNB)
    return jnp.take_along_axis(listed, shuffle.astype(jnp.int32), axis=1).astype(jnp.int32)


def draw_log_norm(key, part):
    key = jax.random.fold_in(key, 5)
    shift = jnp.clip(0.3 * jax.random.normal(key, (H, TOKENS), jnp.float32), -0.9, 0.9)
    return 8.0 + shift


def block_scale(rng, extent, pieces, smallest, high):
    level = 1.0
    for position, shards_of in pieces:
        steps = jax.random.uniform(jax.random.fold_in(jax.random.fold_in(rng, 6), position), (shards_of,), jnp.float32, smallest / len(pieces), high / len(pieces))
        level = level * jnp.repeat(jnp.exp(steps), extent[position] // shards_of).reshape((-1,) + (1,) * (len(extent) - 1 - position))
    return level


def bell_draw(key, dims, scale, bound, pieces=(), kind=jnp.bfloat16):
    result = jax.random.normal(key, dims, jnp.float32) * scale
    if len(pieces) > 0:
        result = block_scale(key, dims, pieces, -0.22, 0.18) * result
    return jnp.clip(result, min=-bound, max=bound).astype(kind)


def setup_inputs(seed: int = 0, part: int = 0) -> dict:
    streams_of = jax.random.split(jax.random.key(seed), 8)
    part_keys = jax.random.split(jax.random.fold_in(streams_of[7], part), 8)
    return {
        "queries": bell_draw(part_keys[0], (TOKENS, D), 1.0, 6.0, ((0, 16),)),
        "keys": bell_draw(part_keys[1], (TOKENS, D), 1.0, 6.0, ((0, 16),)),
        "values": bell_draw(part_keys[2], (TOKENS, D), 1.0, 6.0, ((0, 16),)),
        "outputs": bell_draw(part_keys[3], (TOKENS, D), 1.0, 6.0, ((0, 16),)),
        "out_grad": bell_draw(part_keys[4], (TOKENS, D), 32.0, 192.0, ((0, 16),)),
        "log_norm": draw_log_norm(jax.random.fold_in(jax.random.fold_in(streams_of[7], part), 71), part),
        "contacts": draw_contacts(jax.random.fold_in(jax.random.fold_in(streams_of[7], part), 71), part),
    }


def reference(queries, keys, values, outputs, out_grad, log_norm, contacts):
    token_count, model_width = queries.shape
    head_count = log_norm.shape[0]
    head_dim = model_width // head_count
    score_scale = 1.0 / math.sqrt(head_dim)
    block_count = token_count // BLOCK
    products = out_grad.astype(jnp.float32) * outputs.astype(jnp.float32)
    delta = lax.optimization_barrier(jnp.sum(products.reshape(token_count, head_count, head_dim), axis=2)).T
    key_blocks = keys.reshape(block_count, BLOCK, model_width)
    value_blocks = values.reshape(block_count, BLOCK, model_width)

    def per_block(carry, block_index):
        key_acc, value_acc = carry
        first_row = (block_index * BLOCK).astype(jnp.int32)
        q_block = lax.dynamic_slice_in_dim(queries, first_row, BLOCK, 0)
        grad_block = lax.dynamic_slice_in_dim(out_grad, first_row, BLOCK, 0)
        lse_block = lax.dynamic_slice_in_dim(log_norm, first_row, BLOCK, 1)
        delta_block = lax.dynamic_slice_in_dim(delta, first_row, BLOCK, 1)
        chosen = contacts[block_index]
        near_keys = key_blocks[chosen].reshape(KNB * BLOCK, head_count, head_dim).astype(jnp.float32)
        near_values = value_blocks[chosen].reshape(KNB * BLOCK, head_count, head_dim).astype(jnp.float32)
        q_heads = q_block.reshape(BLOCK, head_count, head_dim).astype(jnp.float32)
        grad_heads = grad_block.reshape(BLOCK, head_count, head_dim).astype(jnp.float32)
        scores = jnp.einsum('qhd,khd->hqk', q_heads, near_keys) * score_scale
        weights = jnp.exp(scores - lse_block[:, :, None])
        weights_b = lax.optimization_barrier(weights.astype(jnp.bfloat16)).astype(jnp.float32)
        payload_slice = jnp.einsum('hqk,qhd->khd', weights_b, grad_heads)
        prob_grad = jnp.einsum('qhd,khd->hqk', grad_heads, near_values)
        score_grad = (weights * (prob_grad - delta_block[:, :, None]) * score_scale).astype(jnp.bfloat16)
        score_grad = lax.optimization_barrier(score_grad).astype(jnp.float32)
        query_portion = jnp.einsum('hqk,khd->qhd', score_grad, near_keys).reshape(BLOCK, model_width)
        key_part = jnp.einsum('hqk,qhd->khd', score_grad, q_heads)
        key_acc = key_acc.at[chosen].add(key_part.reshape(KNB, BLOCK, model_width))
        value_acc = value_acc.at[chosen].add(payload_slice.reshape(KNB, BLOCK, model_width))
        return ((key_acc, value_acc), query_portion.astype(jnp.bfloat16))
    empty = jnp.zeros((block_count, BLOCK, model_width), jnp.float32)
    (key_acc, value_acc), query_parts = lax.scan(per_block, (empty, empty), jnp.arange(block_count, dtype=jnp.int32))
    query_grads = query_parts.reshape(token_count, model_width)
    key_grads = key_acc.reshape(token_count, model_width).astype(jnp.bfloat16)
    value_grads = value_acc.reshape(token_count, model_width).astype(jnp.bfloat16)
    return (query_grads, key_grads, value_grads)
```

```python
import math

import jax
import jax.numpy as jnp
from jax import lax
from jax.experimental import pallas as pl
from jax.experimental.pallas import tpu as pltpu
from jax.sharding import Mesh
from jax.sharding import PartitionSpec as P

BLOCK = 128
LANES = 128
HEADS = 8
STATS = 16
GROUP = 4
NT = (((1,), (1,)), ((), ()))
NN = (((1,), (0,)), ((), ()))
VMEM = pl.BlockSpec(memory_space=pltpu.VMEM)
SMEM = pl.BlockSpec(memory_space=pltpu.SMEM)


def split_three(x):
    hi = x.astype(jnp.bfloat16).astype(jnp.float32)
    rest = x - hi
    mid = rest.astype(jnp.bfloat16).astype(jnp.float32)
    return hi, mid, rest - mid


def pack_kernel(where_ref, contacts_ref, q_ref, k_ref, v_ref, o_ref, g_ref, norm_ref, *rest):
    outs, messages = rest[:HEADS], rest[HEADS]
    width = q_ref.shape[1]
    head_dim = width // HEADS
    me, column = where_ref[0], where_ref[1]
    products = g_ref[...].astype(jnp.float32) * o_ref[...].astype(jnp.float32)
    hi = products.astype(jnp.bfloat16)
    lo = (products - hi.astype(jnp.float32)).astype(jnp.bfloat16)
    owner = lax.broadcasted_iota(jnp.int32, (HEADS, width), 1) // head_dim
    picks = (owner == lax.broadcasted_iota(jnp.int32, (HEADS, width), 0)).astype(jnp.bfloat16)
    delta = lax.dot_general(picks, hi, NT, preferred_element_type=jnp.float32)
    delta += lax.dot_general(picks, lo, NT, preferred_element_type=jnp.float32)
    lane = lax.broadcasted_iota(jnp.int32, (1, LANES), 1)
    listed = jnp.zeros((1, LANES), jnp.float32)
    for i in range(contacts_ref.shape[1]):
        listed = jnp.where(lane == i, contacts_ref[column, i].astype(jnp.float32), listed)
    norm_parts = split_three(norm_ref[...])
    delta_parts = split_three(delta)
    blank = jnp.zeros((STATS - 7, LANES), jnp.float32)
    for h in range(HEADS):
        cols = slice(h * head_dim, (h + 1) * head_dim)
        rows = [part[h : h + 1] for part in norm_parts + delta_parts]
        stats = jnp.concatenate(rows + [listed, blank], axis=0).astype(jnp.bfloat16)
        messages[h, :BLOCK, :] = jnp.concatenate([k_ref[:, cols], v_ref[:, cols]], axis=1)
        messages[h, BLOCK : 2 * BLOCK, :] = jnp.concatenate([q_ref[:, cols], g_ref[:, cols]], axis=1)
        messages[h, 2 * BLOCK :, :] = stats
    for s in range(HEADS):
        outs[s][...] = messages[me ^ s]


def attend_kernel(sizes, where_ref, *rest):
    shares, across, columns, contact_count = sizes
    rows = rest[:HEADS]
    (other_ref, mine_ref, theirs_ref, dq_ref, kv, kt, weights, total, listed, places, sem) = rest[HEADS:]
    me, share = where_ref[0], where_ref[1]
    head_dim = LANES // 2
    score_scale = 1.0 / math.sqrt(head_dim)
    count = shares * HEADS
    for s in range(HEADS):
        kv[s] = rows[s][:BLOCK, :]
        listed[s : s + 1, :] = rows[s][2 * BLOCK :, :].astype(jnp.float32)[6:7].astype(jnp.int32)
    block = listed[...]
    col = block // (across * shares)
    rem = block - col * (across * shares)
    first = rem // shares
    second = rem - first * shares
    slot = (first * columns + col) ^ me
    listed[...] = (second ^ share) * HEADS + slot
    copy = pltpu.make_async_copy(listed, places, sem)
    copy.start()
    for j in range(count - HEADS):
        kv[HEADS + j] = other_ref[j * BLOCK : (j + 1) * BLOCK, :]
    total[...] = jnp.zeros_like(total)
    for j in range(count):
        kt[j] = kv[j].astype(jnp.float32).T[:head_dim, :].astype(jnp.bfloat16)
    low = lax.broadcasted_iota(jnp.int32, (BLOCK, LANES), 1) < head_dim
    for s in range(HEADS):
        both = rows[s][BLOCK : 2 * BLOCK, :]
        weights[s, :BLOCK, :] = jnp.where(low, both, jnp.zeros_like(both))
        weights[s, BLOCK:, :] = jnp.where(low, jnp.zeros_like(both), both)
    copy.wait()
    factor = score_scale * math.log2(math.e)
    for s in range(HEADS):
        stats = rows[s][2 * BLOCK :, :].astype(jnp.float32)
        norm = (stats[0:1] + stats[1:2] + stats[2:3]) * math.log2(math.e)
        delta = stats[3:4] + stats[4:5] + stats[5:6]
        weight = weights[s]
        dq = jnp.zeros((head_dim, BLOCK), jnp.float32)
        for t in range(0, contact_count, GROUP):
            spots = [places[s, t + i] for i in range(min(GROUP, contact_count - t))]
            keys = jnp.concatenate([kv[i] for i in spots], axis=0)
            pair = lax.dot_general(keys, weight, NT, preferred_element_type=jnp.float32)
            probs = jnp.exp2(pair[:, :BLOCK] * factor - norm)
            slope = (probs * (pair[:, BLOCK:] - delta)).astype(jnp.bfloat16)
            joined = jnp.concatenate([slope, probs.astype(jnp.bfloat16)], axis=1)
            grads = lax.dot_general(joined, weight, NN, preferred_element_type=jnp.float32)
            for n, i in enumerate(spots):
                total[i] += grads[n * BLOCK : (n + 1) * BLOCK]
            flat = jnp.concatenate([kt[i] for i in spots], axis=1)
            dq += lax.dot_general(flat, slope, NN, preferred_element_type=jnp.float32)
        dq_ref[s] = (dq * score_scale).astype(jnp.bfloat16)
    final = jnp.where(lax.broadcasted_iota(jnp.int32, (1, LANES), 1) < head_dim, score_scale, 1.0)
    for s in range(HEADS):
        mine_ref[s] = total[s] * final
    for j in range(count - HEADS):
        theirs_ref[j] = (total[HEADS + j] * final).astype(theirs_ref.dtype)


def join_kernel(mine_ref, theirs_ref, dq_ref, *outs):
    for s in range(HEADS):
        both = mine_ref[s] + theirs_ref[s].astype(jnp.float32)
        outs[s][:BLOCK, :] = both.astype(jnp.bfloat16)
        outs[s][BLOCK:, :] = dq_ref[s]


def unpack_kernel(where_ref, *rest):
    parts = rest[:HEADS]
    dq_ref, dk_ref, dv_ref, messages = rest[HEADS:]
    me = where_ref[0]
    head_dim = LANES // 2
    for s in range(HEADS):
        messages[me ^ s] = parts[s][...]
    for h in range(0, HEADS, 2):
        cols = slice(h * head_dim, (h + 2) * head_dim)
        even, odd = messages[h, :BLOCK, :], messages[h + 1, :BLOCK, :]
        dk_ref[:, cols] = jnp.concatenate([even[:, :head_dim], odd[:, :head_dim]], axis=1)
        dv_ref[:, cols] = jnp.concatenate([even[:, head_dim:], odd[:, head_dim:]], axis=1)
        turned = jnp.concatenate([messages[h, BLOCK:, :], messages[h + 1, BLOCK:, :]], axis=0)
        dq_ref[:, cols] = turned.astype(jnp.float32).T.astype(jnp.bfloat16)


def exchange(parts, peers):
    names = ("across", "col")
    moved = [parts[0]]
    for s in range(1, peers):
        moved.append(lax.ppermute(parts[s], names, [(j, j ^ s) for j in range(peers)]))
    return moved


def body(queries, keys, values, outputs, out_grad, log_norm, contacts):
    bf16, f32 = jnp.bfloat16, jnp.float32
    width = queries.shape[1]
    columns = lax.axis_size("col")
    across = lax.axis_size("across")
    shares = lax.axis_size("share")
    contact_count = contacts.shape[1]
    count = shares * HEADS
    column = lax.axis_index("col")
    me = lax.axis_index("across") * columns + column
    share = lax.axis_index("share")
    swap = shares == 2
    params = pltpu.CompilerParams(vmem_limit_bytes=48 * 1024 * 1024)
    length = 2 * BLOCK + STATS
    packed = pl.pallas_call(
        pack_kernel,
        out_shape=[jax.ShapeDtypeStruct((length, LANES), bf16)] * HEADS,
        in_specs=[SMEM, SMEM] + [VMEM] * 6,
        out_specs=[VMEM] * HEADS,
        scratch_shapes=[pltpu.VMEM((HEADS, length, LANES), bf16)],
        compiler_params=params,
    )(jnp.stack([me, column]).astype(jnp.int32), contacts, queries, keys, values, outputs, out_grad, log_norm)
    moved = exchange(packed, HEADS)
    own = jnp.concatenate([m[:BLOCK] for m in moved], axis=0)
    if swap:
        other = lax.ppermute(own, "share", [(0, 1), (1, 0)])
    else:
        gathered = lax.all_gather(own, "share", axis=0, tiled=False)
        turn = (jnp.arange(1, shares) ^ share).astype(jnp.int32)
        other = gathered[turn].reshape(-1, LANES)
    mine, theirs, dq = pl.pallas_call(
        lambda *refs: attend_kernel((shares, across, columns, contact_count), *refs),
        out_shape=[
            jax.ShapeDtypeStruct((HEADS, BLOCK, LANES), f32),
            jax.ShapeDtypeStruct((count - HEADS, BLOCK, LANES), bf16),
            jax.ShapeDtypeStruct((HEADS, LANES // 2, BLOCK), bf16),
        ],
        in_specs=[SMEM] + [VMEM] * (HEADS + 1),
        out_specs=[VMEM] * 3,
        scratch_shapes=[
            pltpu.VMEM((count, BLOCK, LANES), bf16),
            pltpu.VMEM((count, LANES // 2, BLOCK), bf16),
            pltpu.VMEM((HEADS, 2 * BLOCK, LANES), bf16),
            pltpu.VMEM((count, BLOCK, LANES), f32),
            pltpu.VMEM((HEADS, LANES), jnp.int32),
            pltpu.SMEM((HEADS, LANES), jnp.int32),
            pltpu.SemaphoreType.DMA,
        ],
        compiler_params=params,
    )(jnp.stack([me, share]).astype(jnp.int32), *moved, other)
    if swap:
        arrived = lax.ppermute(theirs, "share", [(0, 1), (1, 0)])
    else:
        full = jnp.zeros((shares, HEADS, BLOCK, LANES), f32)
        turn = (jnp.arange(1, shares) ^ share).astype(jnp.int32)
        full = full.at[turn].set(theirs.reshape(shares - 1, HEADS, BLOCK, LANES).astype(f32))
        arrived = lax.psum_scatter(full, "share", scatter_dimension=0, tiled=False)
    joined = pl.pallas_call(
        join_kernel,
        out_shape=[jax.ShapeDtypeStruct((BLOCK + LANES // 2, LANES), bf16)] * HEADS,
        in_specs=[VMEM] * 3,
        out_specs=[VMEM] * HEADS,
        compiler_params=params,
    )(mine, arrived, dq)
    back = exchange(joined, HEADS)
    return pl.pallas_call(
        unpack_kernel,
        out_shape=[jax.ShapeDtypeStruct((BLOCK, width), bf16)] * 3,
        in_specs=[SMEM] + [VMEM] * HEADS,
        out_specs=[VMEM] * 3,
        scratch_shapes=[pltpu.VMEM((HEADS, BLOCK + LANES // 2, LANES), bf16)],
        compiler_params=params,
    )(jnp.stack([me]).astype(jnp.int32), *back)


def solution(mesh):
    groups, rows, columns = (mesh.shape[a] for a in ("groups", "row", "col"))
    across = HEADS // columns
    shape = (groups, across, rows // across, columns)
    split = Mesh(mesh.devices.reshape(shape), ("groups", "across", "share", "col"))
    query_side = ("groups", "across", "share", "col")
    key_side = ("groups", "col", "across", "share")
    in_specs = (
        P(query_side, None),
        P(key_side, None),
        P(key_side, None),
        P(query_side, None),
        P(query_side, None),
        P(None, query_side),
        P(("groups", "across", "share"), None),
    )
    out_specs = (P(query_side, None), P(key_side, None), P(key_side, None))
    return jax.shard_map(body, mesh=split, in_specs=in_specs, out_specs=out_specs, check_vma=False)
```

```python
import math

import jax
import jax.numpy as jnp
from jax import lax
from jax.experimental import pallas as pl
from jax.experimental.pallas import tpu as pltpu
from jax.sharding import Mesh
from jax.sharding import PartitionSpec as P

BLOCK = 128
LANES = 128
HEADS = 8
STATS = 16
GROUP = 12
NT = (((1,), (1,)), ((), ()))
NN = (((1,), (0,)), ((), ()))
VMEM = pl.BlockSpec(memory_space=pltpu.VMEM)
SMEM = pl.BlockSpec(memory_space=pltpu.SMEM)
HBM = pl.BlockSpec(memory_space=pltpu.HBM)
ORDER_OUT = (2, 4, 7, 5, 6, 1, 3)
ORDER_BACK = (3, 2, 6, 7, 5, 4, 1)


def split_three(x):
    hi = x.astype(jnp.bfloat16).astype(jnp.float32)
    rest = x - hi
    mid = rest.astype(jnp.bfloat16).astype(jnp.float32)
    return hi, mid, rest - mid


def pack_kernel(where_ref, contacts_hbm, *rest):
    sources, outs = rest[:6], rest[6 : 6 + HEADS]
    messages, contacts_ref, q_ref, k_ref, v_ref, o_ref, g_ref, norm_ref, sems = rest[6 + HEADS :]
    targets = (q_ref, k_ref, v_ref, o_ref, g_ref, norm_ref)
    copies = [pltpu.make_async_copy(a, b, sems.at[i]) for i, (a, b) in enumerate(zip(sources, targets))]
    copies.append(pltpu.make_async_copy(contacts_hbm, contacts_ref, sems.at[6]))
    for i in (4, 3, 5, 6, 0, 1, 2):
        copies[i].start()
    width = q_ref.shape[1]
    head_dim = width // HEADS
    me, column = where_ref[0], where_ref[1]
    for i in (4, 3, 5, 6):
        copies[i].wait()
    products = g_ref[...].astype(jnp.float32) * o_ref[...].astype(jnp.float32)
    hi = products.astype(jnp.bfloat16)
    lo = (products - hi.astype(jnp.float32)).astype(jnp.bfloat16)
    owner = lax.broadcasted_iota(jnp.int32, (HEADS, width), 1) // head_dim
    picks = (owner == lax.broadcasted_iota(jnp.int32, (HEADS, width), 0)).astype(jnp.bfloat16)
    delta = lax.dot_general(picks, hi, NT, preferred_element_type=jnp.float32)
    delta += lax.dot_general(picks, lo, NT, preferred_element_type=jnp.float32)
    lane = lax.broadcasted_iota(jnp.int32, (1, LANES), 1)
    listed = jnp.zeros((1, LANES), jnp.float32)
    for i in range(contacts_ref.shape[1]):
        listed = jnp.where(lane == i, contacts_ref[column, i].astype(jnp.float32), listed)
    norm_parts = split_three(norm_ref[...])
    delta_parts = split_three(delta)
    for i in (0, 1, 2):
        copies[i].wait()
    blank = jnp.zeros((STATS - 7, LANES), jnp.float32)
    for h in range(HEADS):
        cols = slice(h * head_dim, (h + 1) * head_dim)
        rows = [part[h : h + 1] for part in norm_parts + delta_parts]
        stats = jnp.concatenate(rows + [listed, blank], axis=0).astype(jnp.bfloat16)
        messages[h, :BLOCK, :] = jnp.concatenate([k_ref[:, cols], v_ref[:, cols]], axis=1)
        messages[h, BLOCK : 2 * BLOCK, :] = jnp.concatenate([q_ref[:, cols], g_ref[:, cols]], axis=1)
        messages[h, 2 * BLOCK :, :] = stats
    for s in range(HEADS):
        outs[s][...] = messages[me ^ s]


def attend_kernel(sizes, where_ref, *rest):
    shares, across, columns, contact_count = sizes
    order = (0,) + ORDER_OUT
    rows = [rest[order.index(s)] for s in range(HEADS)]
    (other_ref, mine_ref, theirs_ref, dq_ref, kv, kt, weights, total, listed, places, sem) = rest[HEADS:]
    me, share = where_ref[0], where_ref[1]
    head_dim = LANES // 2
    score_scale = 1.0 / math.sqrt(head_dim)
    count = shares * HEADS
    for s in range(HEADS):
        kv[s] = rows[s][:BLOCK, :]
        listed[s : s + 1, :] = rows[s][2 * BLOCK :, :].astype(jnp.float32)[6:7].astype(jnp.int32)
    block = listed[...]
    col = block // (across * shares)
    rem = block - col * (across * shares)
    first = rem // shares
    second = rem - first * shares
    slot = (first * columns + col) ^ me
    listed[...] = (second ^ share) * HEADS + slot
    copy = pltpu.make_async_copy(listed, places, sem)
    copy.start()
    for j in range(count - HEADS):
        spot = HEADS * (1 + j // HEADS) + order[j % HEADS]
        kv[spot] = other_ref[j * BLOCK : (j + 1) * BLOCK, :]
    total[...] = jnp.zeros_like(total)
    for j in range(count):
        kt[j] = kv[j].astype(jnp.float32).T[:head_dim, :].astype(jnp.bfloat16)
    low = lax.broadcasted_iota(jnp.int32, (BLOCK, LANES), 1) < head_dim
    for s in range(HEADS):
        both = rows[s][BLOCK : 2 * BLOCK, :]
        weights[s, :BLOCK, :] = jnp.where(low, both, jnp.zeros_like(both))
        weights[s, BLOCK:, :] = jnp.where(low, jnp.zeros_like(both), both)
    copy.wait()
    factor = score_scale * math.log2(math.e)
    for s in range(HEADS):
        stats = rows[s][2 * BLOCK :, :].astype(jnp.float32)
        norm = (stats[0:1] + stats[1:2] + stats[2:3]) * math.log2(math.e)
        delta = stats[3:4] + stats[4:5] + stats[5:6]
        weight = weights[s]
        dq = jnp.zeros((head_dim, BLOCK), jnp.float32)
        for t in range(0, contact_count, GROUP):
            spots = [places[s, t + i] for i in range(min(GROUP, contact_count - t))]
            keys = jnp.concatenate([kv[i] for i in spots], axis=0)
            pair = lax.dot_general(keys, weight, NT, preferred_element_type=jnp.float32)
            probs = jnp.exp2(pair[:, :BLOCK] * factor - norm)
            slope = (probs * (pair[:, BLOCK:] - delta)).astype(jnp.bfloat16)
            joined = jnp.concatenate([slope, probs.astype(jnp.bfloat16)], axis=1)
            grads = lax.dot_general(joined, weight, NN, preferred_element_type=jnp.float32)
            for n, i in enumerate(spots):
                total[i] += grads[n * BLOCK : (n + 1) * BLOCK]
            flat = jnp.concatenate([kt[i] for i in spots], axis=1)
            dq += lax.dot_general(flat, slope, NN, preferred_element_type=jnp.float32)
        dq_ref[s] = (dq * score_scale).astype(jnp.bfloat16)
    final = jnp.where(lax.broadcasted_iota(jnp.int32, (1, LANES), 1) < head_dim, score_scale, 1.0)
    for s in range(HEADS):
        mine_ref[s] = total[s] * final
    for j in range(count - HEADS):
        theirs_ref[j] = (total[HEADS + j] * final).astype(theirs_ref.dtype)


def join_kernel(mine_ref, theirs_ref, dq_ref, *outs):
    for s in range(HEADS):
        both = mine_ref[s] + theirs_ref[s].astype(jnp.float32)
        outs[s][:BLOCK, :] = both.astype(jnp.bfloat16)
        outs[s][BLOCK:, :] = dq_ref[s]


def unpack_kernel(where_ref, *rest):
    order = (0,) + ORDER_BACK
    parts = [rest[order.index(s)] for s in range(HEADS)]
    dq_ref, dk_ref, dv_ref, messages = rest[HEADS:]
    me = where_ref[0]
    head_dim = LANES // 2
    for s in range(HEADS):
        messages[me ^ s] = parts[s][...]
    for h in range(0, HEADS, 2):
        cols = slice(h * head_dim, (h + 2) * head_dim)
        even, odd = messages[h, :BLOCK, :], messages[h + 1, :BLOCK, :]
        dk_ref[:, cols] = jnp.concatenate([even[:, :head_dim], odd[:, :head_dim]], axis=1)
        dv_ref[:, cols] = jnp.concatenate([even[:, head_dim:], odd[:, head_dim:]], axis=1)
        turned = jnp.concatenate([messages[h, BLOCK:, :], messages[h + 1, BLOCK:, :]], axis=0)
        dq_ref[:, cols] = turned.astype(jnp.float32).T.astype(jnp.bfloat16)


def exchange(parts, order):
    moved = [parts[0]]
    for s in order:
        pairs = [(j, j ^ s) for j in range(HEADS)]
        moved.append(lax.ppermute(parts[s], ("across", "col"), pairs))
    return moved


def body(queries, keys, values, outputs, out_grad, log_norm, contacts):
    bf16, f32 = jnp.bfloat16, jnp.float32
    width = queries.shape[1]
    columns = lax.axis_size("col")
    across = lax.axis_size("across")
    shares = lax.axis_size("share")
    contact_count = contacts.shape[1]
    count = shares * HEADS
    column = lax.axis_index("col")
    me = lax.axis_index("across") * columns + column
    share = lax.axis_index("share")
    swap = shares == 2
    params = pltpu.CompilerParams(vmem_limit_bytes=48 * 1024 * 1024)
    length = 2 * BLOCK + STATS
    loaded = [
        pltpu.with_memory_space_constraint(a, pltpu.HBM)
        for a in (queries, keys, values, outputs, out_grad, log_norm)
    ]
    packed = pl.pallas_call(
        pack_kernel,
        out_shape=[jax.ShapeDtypeStruct((length, LANES), bf16)] * HEADS,
        in_specs=[SMEM] + [HBM] * 7,
        out_specs=[VMEM] * HEADS,
        scratch_shapes=[
            pltpu.VMEM((HEADS, length, LANES), bf16),
            pltpu.SMEM(contacts.shape, jnp.int32),
            *[pltpu.VMEM(a.shape, a.dtype) for a in loaded],
            pltpu.SemaphoreType.DMA((7,)),
        ],
        compiler_params=params,
    )(jnp.stack([me, column]).astype(jnp.int32), pltpu.with_memory_space_constraint(contacts, pltpu.HBM), *loaded)
    moved = exchange(packed, ORDER_OUT)
    own = jnp.concatenate([m[:BLOCK] for m in moved], axis=0)
    if swap:
        other = lax.ppermute(own, "share", [(0, 1), (1, 0)])
    else:
        gathered = lax.all_gather(own, "share", axis=0, tiled=False)
        turn = (jnp.arange(1, shares) ^ share).astype(jnp.int32)
        other = gathered[turn].reshape(-1, LANES)
    mine, theirs, dq = pl.pallas_call(
        lambda *refs: attend_kernel((shares, across, columns, contact_count), *refs),
        out_shape=[
            jax.ShapeDtypeStruct((HEADS, BLOCK, LANES), f32),
            jax.ShapeDtypeStruct((count - HEADS, BLOCK, LANES), bf16),
            jax.ShapeDtypeStruct((HEADS, LANES // 2, BLOCK), bf16),
        ],
        in_specs=[SMEM] + [VMEM] * (HEADS + 1),
        out_specs=[VMEM] * 3,
        scratch_shapes=[
            pltpu.VMEM((count, BLOCK, LANES), bf16),
            pltpu.VMEM((count, LANES // 2, BLOCK), bf16),
            pltpu.VMEM((HEADS, 2 * BLOCK, LANES), bf16),
            pltpu.VMEM((count, BLOCK, LANES), f32),
            pltpu.VMEM((HEADS, LANES), jnp.int32),
            pltpu.SMEM((HEADS, LANES), jnp.int32),
            pltpu.SemaphoreType.DMA,
        ],
        compiler_params=params,
    )(jnp.stack([me, share]).astype(jnp.int32), *moved, other)
    if swap:
        arrived = lax.ppermute(theirs, "share", [(0, 1), (1, 0)])
    else:
        full = jnp.zeros((shares, HEADS, BLOCK, LANES), f32)
        turn = (jnp.arange(1, shares) ^ share).astype(jnp.int32)
        full = full.at[turn].set(theirs.reshape(shares - 1, HEADS, BLOCK, LANES).astype(f32))
        arrived = lax.psum_scatter(full, "share", scatter_dimension=0, tiled=False)
    joined = pl.pallas_call(
        join_kernel,
        out_shape=[jax.ShapeDtypeStruct((BLOCK + LANES // 2, LANES), bf16)] * HEADS,
        in_specs=[VMEM] * 3,
        out_specs=[VMEM] * HEADS,
        compiler_params=params,
    )(mine, arrived, dq)
    back = exchange(joined, ORDER_BACK)
    return pl.pallas_call(
        unpack_kernel,
        out_shape=[jax.ShapeDtypeStruct((BLOCK, width), bf16)] * 3,
        in_specs=[SMEM] + [VMEM] * HEADS,
        out_specs=[VMEM] * 3,
        scratch_shapes=[pltpu.VMEM((HEADS, BLOCK + LANES // 2, LANES), bf16)],
        compiler_params=params,
    )(jnp.stack([me]).astype(jnp.int32), *back)


def solution(mesh):
    groups, rows, columns = (mesh.shape[a] for a in ("groups", "row", "col"))
    across = HEADS // columns
    shape = (groups, across, rows // across, columns)
    split = Mesh(mesh.devices.reshape(shape), ("groups", "across", "share", "col"))
    query_side = ("groups", "across", "share", "col")
    key_side = ("groups", "col", "across", "share")
    in_specs = (
        P(query_side, None),
        P(key_side, None),
        P(key_side, None),
        P(query_side, None),
        P(query_side, None),
        P(None, query_side),
        P(("groups", "across", "share"), None),
    )
    out_specs = (P(query_side, None), P(key_side, None), P(key_side, None))
    return jax.shard_map(body, mesh=split, in_specs=in_specs, out_specs=out_specs, check_vma=False)
```

```python
import math

import jax
import jax.numpy as jnp
from jax import lax
from jax.experimental import pallas as pl
from jax.experimental.pallas import tpu as pltpu
from jax.sharding import Mesh
from jax.sharding import PartitionSpec as P

BLOCK = 128
LANES = 128
HEADS = 8
STATS = 16
STEP = 2
AHEAD = 3
NT = (((1,), (1,)), ((), ()))
NN = (((1,), (0,)), ((), ()))
VMEM = pl.BlockSpec(memory_space=pltpu.VMEM)
SMEM = pl.BlockSpec(memory_space=pltpu.SMEM)
HBM = pl.BlockSpec(memory_space=pltpu.HBM)
ORDER_OUT = (2, 4, 7, 5, 6, 1, 3)
ORDER_BACK = (3, 2, 6, 7, 5, 4, 1)


def contact_plan(sizes):
    shares, contact_count = sizes[0], sizes[3]
    home = max(0, contact_count - (shares - 1) * HEADS)
    return home // 2, contact_count - home + home // 2, contact_count


def number():
    return lax.axis_index("across") * lax.axis_size("col") + lax.axis_index("col")


def split_three(x):
    hi = x.astype(jnp.bfloat16).astype(jnp.float32)
    rest = x - hi
    mid = rest.astype(jnp.bfloat16).astype(jnp.float32)
    return hi, mid, rest - mid


def listed_contacts(contacts_ref, column, share, sizes):
    shares, across, columns, contact_count = sizes
    start, end, _ = contact_plan(sizes)
    home = start + contact_count - end
    target = lax.broadcasted_iota(jnp.int32, (HEADS, LANES), 0)
    lane = lax.broadcasted_iota(jnp.int32, (HEADS, LANES), 1)
    spots, ranks = [], []
    for i in range(contact_count):
        block = contacts_ref[column, i]
        col = block // (across * shares)
        rem = block - col * (across * shares)
        row = rem // shares
        away = (rem - row * shares) ^ share
        spots.append(away * HEADS + (target ^ (row * columns + col)))
        ranks.append(jnp.where(away == 0, 0, contact_count) + i)
    listed = jnp.zeros((HEADS, LANES), jnp.int32)
    for i in range(contact_count):
        rank = sum((ranks[j] < ranks[i]).astype(jnp.int32) for j in range(contact_count) if j != i)
        after = jnp.where(rank < home, rank + end - start, rank - home + start)
        listed = jnp.where(lane == jnp.where(rank < start, rank, after), spots[i], listed)
    return listed


def pack_kernel(sizes, contacts_hbm, *rest):
    sources, outs = rest[:6], rest[6 : 6 + HEADS]
    messages, contacts_ref, q_ref, k_ref, v_ref, o_ref, g_ref, norm_ref, sems = rest[6 + HEADS :]
    targets = (q_ref, k_ref, v_ref, o_ref, g_ref, norm_ref)
    copies = [pltpu.make_async_copy(a, b, sems.at[i]) for i, (a, b) in enumerate(zip(sources, targets))]
    copies.append(pltpu.make_async_copy(contacts_hbm, contacts_ref, sems.at[6]))
    for i in (6, 4, 3, 5, 0, 1, 2):
        copies[i].start()
    width = q_ref.shape[1]
    head_dim = width // HEADS
    me, column, share = number(), lax.axis_index("col"), lax.axis_index("share")
    copies[6].wait()
    listed = listed_contacts(contacts_ref, column, share, sizes).astype(jnp.float32)
    for i in (4, 3, 5):
        copies[i].wait()
    products = g_ref[...].astype(jnp.float32) * o_ref[...].astype(jnp.float32)
    hi = products.astype(jnp.bfloat16)
    lo = (products - hi.astype(jnp.float32)).astype(jnp.bfloat16)
    owner = lax.broadcasted_iota(jnp.int32, (HEADS, width), 1) // head_dim
    picks = (owner == lax.broadcasted_iota(jnp.int32, (HEADS, width), 0)).astype(jnp.bfloat16)
    delta = lax.dot_general(picks, hi, NT, preferred_element_type=jnp.float32)
    delta += lax.dot_general(picks, lo, NT, preferred_element_type=jnp.float32)
    norm_parts = split_three(norm_ref[...])
    delta_parts = split_three(delta)
    for i in (0, 1, 2):
        copies[i].wait()
    blank = jnp.zeros((STATS - 7, LANES), jnp.float32)
    for h in range(HEADS):
        cols = slice(h * head_dim, (h + 1) * head_dim)
        rows = [part[h : h + 1] for part in (listed,) + norm_parts + delta_parts]
        stats = jnp.concatenate(rows + [blank], axis=0).astype(jnp.bfloat16)
        messages[h, :BLOCK, :] = jnp.concatenate([k_ref[:, cols], v_ref[:, cols]], axis=1)
        messages[h, BLOCK : 2 * BLOCK, :] = jnp.concatenate([q_ref[:, cols], g_ref[:, cols]], axis=1)
        messages[h, 2 * BLOCK :, :] = stats
    for s in range(HEADS):
        outs[s][...] = messages[me ^ s]


def fill_turned(kt, kv, j):
    kt[j] = kv[j].astype(jnp.float32).T[: LANES // 2, :].astype(jnp.bfloat16)


def fill_weight(weight, both):
    low = lax.broadcasted_iota(jnp.int32, (BLOCK, LANES), 1) < LANES // 2
    weight[:BLOCK, :] = jnp.where(low, both, jnp.zeros_like(both))
    weight[BLOCK:, :] = jnp.where(low, jnp.zeros_like(both), both)


def by_slot(refs):
    order = (0,) + ORDER_OUT
    return [refs[order.index(s)] for s in range(HEADS)]


def lists_of(rows):
    taken = [row[2 * BLOCK :, :].astype(jnp.float32)[0:1] for row in rows]
    return jnp.concatenate(taken, axis=0).astype(jnp.int32)


def run(jobs, kv, kt, total):
    head_dim = LANES // 2
    factor = math.log2(math.e) / math.sqrt(head_dim)
    steps = [(n, job[2][t : t + STEP]) for n, job in enumerate(jobs) for t in range(0, len(job[2]), STEP)]
    pairs, probabilities = {}, {}
    sums = [jnp.zeros((head_dim, BLOCK), jnp.float32) for _ in jobs]

    def score(x):
        n, spots = steps[x]
        block = jnp.concatenate([kv[i] for i in spots], axis=0)
        pairs[x] = lax.dot_general(block, jobs[n][1][...], NT, preferred_element_type=jnp.float32)

    def soften(x):
        stats = jobs[steps[x][0]][0][2 * BLOCK :, :].astype(jnp.float32)
        norm = (stats[1:2] + stats[2:3] + stats[3:4]) * math.log2(math.e)
        delta = stats[4:5] + stats[5:6] + stats[6:7]
        pair = pairs.pop(x)
        probs = jnp.exp2(pair[:, :BLOCK] * factor - norm)
        slope = (probs * (pair[:, BLOCK:] - delta)).astype(jnp.bfloat16)
        probabilities[x] = (slope, probs.astype(jnp.bfloat16))

    def spread(x):
        n, spots = steps[x]
        slope, probs = probabilities.pop(x)
        joined = jnp.concatenate([slope, probs], axis=1)
        grads = lax.dot_general(joined, jobs[n][1][...], NN, preferred_element_type=jnp.float32)
        for m, i in enumerate(spots):
            total[i] += grads[m * BLOCK : (m + 1) * BLOCK]
        flat = jnp.concatenate([kt[i] for i in spots], axis=1)
        sums[n] += lax.dot_general(flat, slope, NN, preferred_element_type=jnp.float32)

    for x in range(len(steps) + AHEAD + 1):
        if x < len(steps):
            score(x)
        if 0 <= x - AHEAD < len(steps):
            soften(x - AHEAD)
        if 0 <= x - AHEAD - 1:
            spread(x - AHEAD - 1)
    return sums


def first_kernel(sizes, *rest):
    rows = by_slot(rest[:HEADS])
    kv, kt, weights, total, dq = rest[HEADS:]
    start = contact_plan(sizes)[0]
    lists = lists_of(rows)
    total[...] = jnp.zeros_like(total)
    for s in range(HEADS):
        kv[s] = rows[s][:BLOCK, :]
        fill_turned(kt, kv, s)
        fill_weight(weights.at[s], rows[s][BLOCK : 2 * BLOCK, :])
    jobs = [(rows[s], weights.at[s], [lists[s, i] for i in range(start)]) for s in range(HEADS)]
    for s, part in enumerate(run(jobs, kv, kt, total)):
        dq[s] = part


def second_kernel(sizes, *rest):
    rows = by_slot(rest[:HEADS])
    other_ref, _, _, weights, _, _, kv, kt, total, dq, theirs_ref = rest[HEADS:]
    start, end, _ = contact_plan(sizes)
    lists = lists_of(rows)
    order = (0,) + ORDER_OUT
    for j in range((sizes[0] - 1) * HEADS):
        spot = HEADS * (1 + j // HEADS) + order[j % HEADS]
        kv[spot] = other_ref[j * BLOCK : (j + 1) * BLOCK, :]
        fill_turned(kt, kv, spot)
    jobs = [(rows[s], weights.at[s], [lists[s, i] for i in range(start, end)]) for s in range(HEADS)]
    for s, part in enumerate(run(jobs, kv, kt, total)):
        dq[s] += part
    final = final_scale()
    for j in range(theirs_ref.shape[0]):
        theirs_ref[j] = (total[HEADS + j] * final).astype(theirs_ref.dtype)


def third_kernel(sizes, *rest):
    rows = by_slot(rest[:HEADS])
    kv, kt, weights, total_in, dq_in, mine_ref, dq_ref, total = rest[HEADS:]
    _, start, end = contact_plan(sizes)
    lists = lists_of(rows)
    for s in range(HEADS):
        total[s] = total_in[s]
    jobs = [(rows[s], weights.at[s], [lists[s, i] for i in range(start, end)]) for s in range(HEADS)]
    for s, part in enumerate(run(jobs, kv, kt, total)):
        dq_ref[s] = ((dq_in[s] + part) / math.sqrt(LANES // 2)).astype(jnp.bfloat16)
    final = final_scale()
    for s in range(HEADS):
        mine_ref[s] = total[s] * final


def final_scale():
    lane = lax.broadcasted_iota(jnp.int32, (1, LANES), 1)
    return jnp.where(lane < LANES // 2, 1.0 / math.sqrt(LANES // 2), 1.0)


def join_kernel(mine_ref, theirs_ref, dq_ref, *outs):
    for s in range(HEADS):
        both = mine_ref[s] + theirs_ref[s].astype(jnp.float32)
        outs[s][:BLOCK, :] = both.astype(jnp.bfloat16)
        outs[s][BLOCK:, :] = dq_ref[s]


def unpack_kernel(*rest):
    order = (0,) + ORDER_BACK
    parts = [rest[order.index(s)] for s in range(HEADS)]
    dq_ref, dk_ref, dv_ref, messages = rest[HEADS:]
    me = number()
    head_dim = LANES // 2
    for s in range(HEADS):
        messages[me ^ s] = parts[s][...]
    for h in range(0, HEADS, 2):
        cols = slice(h * head_dim, (h + 2) * head_dim)
        even, odd = messages[h, :BLOCK, :], messages[h + 1, :BLOCK, :]
        dk_ref[:, cols] = jnp.concatenate([even[:, :head_dim], odd[:, :head_dim]], axis=1)
        dv_ref[:, cols] = jnp.concatenate([even[:, head_dim:], odd[:, head_dim:]], axis=1)
        turned = jnp.concatenate([messages[h, BLOCK:, :], messages[h + 1, BLOCK:, :]], axis=0)
        dq_ref[:, cols] = turned.astype(jnp.float32).T.astype(jnp.bfloat16)


def exchange(parts, order):
    moved = {0: parts[0]}
    for s in order:
        pairs = [(j, j ^ s) for j in range(HEADS)]
        moved[s] = lax.ppermute(parts[s], ("across", "col"), pairs)
    return moved


def gather_keys(own, shares, share):
    if shares == 2:
        return lax.ppermute(own, "share", [(0, 1), (1, 0)])
    gathered = lax.all_gather(own, "share", axis=0, tiled=False)
    return gathered[jnp.arange(1, shares) ^ share].reshape(-1, LANES)


def sum_shares(theirs, shares, share):
    if shares == 2:
        return lax.ppermute(theirs, "share", [(0, 1), (1, 0)])
    full = jnp.zeros((shares, HEADS, BLOCK, LANES), jnp.float32)
    parts = theirs.reshape(shares - 1, HEADS, BLOCK, LANES).astype(jnp.float32)
    full = full.at[jnp.arange(1, shares) ^ share].set(parts)
    return lax.psum_scatter(full, "share", scatter_dimension=0, tiled=False)


def call(kernel, outs, in_specs, scratch=(), tiles=0, aliases=None):
    flops = tiles * 10 * BLOCK * BLOCK * (LANES // 2)
    cost = pl.CostEstimate(flops=flops, bytes_accessed=1 << 20, transcendentals=tiles * BLOCK * BLOCK)
    return pl.pallas_call(
        kernel,
        out_shape=[jax.ShapeDtypeStruct(shape, dtype) for shape, dtype in outs],
        in_specs=in_specs,
        out_specs=[VMEM] * len(outs),
        scratch_shapes=list(scratch),
        cost_estimate=cost if tiles else None,
        input_output_aliases=aliases or {},
        compiler_params=pltpu.CompilerParams(vmem_limit_bytes=48 * 1024 * 1024),
    )


def body(queries, keys, values, outputs, out_grad, log_norm, contacts):
    bf16, f32 = jnp.bfloat16, jnp.float32
    width = queries.shape[1]
    columns = lax.axis_size("col")
    across = lax.axis_size("across")
    shares = lax.axis_size("share")
    contact_count = contacts.shape[1]
    sizes = (shares, across, columns, contact_count)
    count = shares * HEADS
    half = LANES // 2
    share = lax.axis_index("share")
    length = 2 * BLOCK + STATS
    loaded = [
        pltpu.with_memory_space_constraint(a, pltpu.HBM)
        for a in (contacts, queries, keys, values, outputs, out_grad, log_norm)
    ]
    packed = call(
        lambda *refs: pack_kernel(sizes, *refs),
        [((length, LANES), bf16)] * HEADS,
        [HBM] * 7,
        [
            pltpu.VMEM((HEADS, length, LANES), bf16),
            pltpu.SMEM(contacts.shape, jnp.int32),
            *[pltpu.VMEM(a.shape, a.dtype) for a in loaded[1:]],
            pltpu.SemaphoreType.DMA((7,)),
        ],
    )(*loaded)
    moved = exchange(packed, ORDER_OUT)
    order = (0,) + ORDER_OUT
    rows = [moved[s] for s in order]
    start, end, _ = contact_plan(sizes)
    own = jnp.concatenate([row[:BLOCK] for row in rows], axis=0)
    other = gather_keys(own, shares, share)
    held = [
        ((count, BLOCK, LANES), bf16),
        ((count, half, LANES), bf16),
        ((HEADS, 2 * BLOCK, LANES), bf16),
        ((count, BLOCK, LANES), f32),
        ((HEADS, half, BLOCK), f32),
    ]
    kv, kt, weights, total, dq = call(
        lambda *refs: first_kernel(sizes, *refs),
        held,
        [VMEM] * HEADS,
        tiles=HEADS * start + 12,
    )(*rows)
    kv, kt, total, dq, theirs = call(
        lambda *refs: second_kernel(sizes, *refs),
        [held[0], held[1], held[3], held[4], ((count - HEADS, BLOCK, LANES), bf16)],
        [VMEM] * (HEADS + 6),
        tiles=HEADS * (end - start),
        aliases={HEADS + 1: 0, HEADS + 2: 1, HEADS + 4: 2, HEADS + 5: 3},
    )(*rows, other, kv, kt, weights, total, dq)
    arrived = sum_shares(theirs, shares, share)
    mine, dq = call(
        lambda *refs: third_kernel(sizes, *refs),
        [((HEADS, BLOCK, LANES), f32), ((HEADS, half, BLOCK), bf16)],
        [VMEM] * (HEADS + 5),
        [pltpu.VMEM((HEADS, BLOCK, LANES), f32)],
        tiles=HEADS * (contact_count - end) + 1,
    )(*rows, kv, kt, weights, total, dq)
    joined = call(
        join_kernel,
        [((BLOCK + half, LANES), bf16)] * HEADS,
        [VMEM] * 3,
    )(mine, arrived, dq)
    back = exchange(joined, ORDER_BACK)
    return call(
        unpack_kernel,
        [((BLOCK, width), bf16)] * 3,
        [VMEM] * HEADS,
        [pltpu.VMEM((HEADS, BLOCK + half, LANES), bf16)],
    )(*[back[s] for s in (0,) + ORDER_BACK])


def solution(mesh):
    groups, rows, columns = (mesh.shape[a] for a in ("groups", "row", "col"))
    across = HEADS // columns
    shape = (groups, across, rows // across, columns)
    split = Mesh(mesh.devices.reshape(shape), ("groups", "across", "share", "col"))
    query_side = ("groups", "across", "share", "col")
    key_side = ("groups", "col", "across", "share")
    in_specs = (
        P(query_side, None),
        P(key_side, None),
        P(key_side, None),
        P(query_side, None),
        P(query_side, None),
        P(None, query_side),
        P(("groups", "across", "share"), None),
    )
    out_specs = (P(query_side, None), P(key_side, None), P(key_side, None))
    return jax.shard_map(body, mesh=split, in_specs=in_specs, out_specs=out_specs, check_vma=False)
```

```python
import math

import jax
import jax.numpy as jnp
from jax import lax
from jax.experimental import pallas as pl
from jax.experimental.pallas import tpu as pltpu
from jax.sharding import Mesh
from jax.sharding import PartitionSpec as P

BLOCK = 128
LANES = 128
HEADS = 8
STATS = 16
STEP = 2
AHEAD = 3
NT = (((1,), (1,)), ((), ()))
NN = (((1,), (0,)), ((), ()))
VMEM = pl.BlockSpec(memory_space=pltpu.VMEM)
SMEM = pl.BlockSpec(memory_space=pltpu.SMEM)
HBM = pl.BlockSpec(memory_space=pltpu.HBM)
ORDER_OUT = (4, 2, 7, 5, 1, 6, 3)
ORDER_BACK = (3, 2, 6, 7, 5, 4, 1)
LATE = (6, 3)
GROUPS = ((0, 4), (2, 7), (5, 1))
EARLY = sum(GROUPS, ())


def contact_plan(sizes):
    shares, contact_count = sizes[0], sizes[3]
    home = max(0, contact_count - (shares - 1) * HEADS)
    late = len(LATE) * (shares - 1 if home >= len(LATE) else shares)
    away = contact_count - home
    return max(0, away - late), away, away + home // 2, contact_count


def number():
    return lax.axis_index("across") * lax.axis_size("col") + lax.axis_index("col")


def split_three(x):
    hi = x.astype(jnp.bfloat16).astype(jnp.float32)
    rest = x - hi
    mid = rest.astype(jnp.bfloat16).astype(jnp.float32)
    return hi, mid, rest - mid


def listed_contacts(contacts_ref, column, share, sizes):
    shares, across, columns, contact_count = sizes
    away_count = contact_plan(sizes)[1]
    home = contact_count - away_count
    target = lax.broadcasted_iota(jnp.int32, (HEADS, LANES), 0)
    lane = lax.broadcasted_iota(jnp.int32, (HEADS, LANES), 1)
    spots, ranks = [], []
    for i in range(contact_count):
        block = contacts_ref[column, i]
        col = block // (across * shares)
        rem = block - col * (across * shares)
        row = rem // shares
        away = (rem - row * shares) ^ share
        slot = target ^ (row * columns + col)
        late = sum((slot == s).astype(jnp.int32) for s in LATE)
        spots.append(away * HEADS + slot)
        ranks.append(jnp.where(away == 0, -late, 2 + late) * contact_count + i)
    listed = jnp.zeros((HEADS, LANES), jnp.int32)
    for i in range(contact_count):
        rank = sum((ranks[j] < ranks[i]).astype(jnp.int32) for j in range(contact_count) if j != i)
        place = jnp.where(rank < home, rank + away_count, rank - home)
        listed = jnp.where(lane == place, spots[i], listed)
    return listed


def pack_kernel(sizes, contacts_hbm, *rest):
    sources, outs = rest[:6], rest[6 : 6 + HEADS]
    messages, contacts_ref, q_ref, k_ref, v_ref, o_ref, g_ref, norm_ref, sems = rest[6 + HEADS :]
    targets = (q_ref, k_ref, v_ref, o_ref, g_ref, norm_ref)
    copies = [pltpu.make_async_copy(a, b, sems.at[i]) for i, (a, b) in enumerate(zip(sources, targets))]
    copies.append(pltpu.make_async_copy(contacts_hbm, contacts_ref, sems.at[6]))
    for i in (6, 4, 3, 5, 0, 1, 2):
        copies[i].start()
    width = q_ref.shape[1]
    head_dim = width // HEADS
    me, column, share = number(), lax.axis_index("col"), lax.axis_index("share")
    copies[6].wait()
    listed = listed_contacts(contacts_ref, column, share, sizes).astype(jnp.float32)
    for i in (4, 3, 5):
        copies[i].wait()
    products = g_ref[...].astype(jnp.float32) * o_ref[...].astype(jnp.float32)
    hi = products.astype(jnp.bfloat16)
    lo = (products - hi.astype(jnp.float32)).astype(jnp.bfloat16)
    owner = lax.broadcasted_iota(jnp.int32, (HEADS, width), 1) // head_dim
    picks = (owner == lax.broadcasted_iota(jnp.int32, (HEADS, width), 0)).astype(jnp.bfloat16)
    delta = lax.dot_general(picks, hi, NT, preferred_element_type=jnp.float32)
    delta += lax.dot_general(picks, lo, NT, preferred_element_type=jnp.float32)
    norm_parts = split_three(norm_ref[...])
    delta_parts = split_three(delta)
    for i in (0, 1, 2):
        copies[i].wait()
    blank = jnp.zeros((STATS - 7, LANES), jnp.float32)
    for h in range(HEADS):
        cols = slice(h * head_dim, (h + 1) * head_dim)
        rows = [part[h : h + 1] for part in (listed,) + norm_parts + delta_parts]
        stats = jnp.concatenate(rows + [blank], axis=0).astype(jnp.bfloat16)
        messages[h, :BLOCK, :] = jnp.concatenate([k_ref[:, cols], v_ref[:, cols]], axis=1)
        messages[h, BLOCK : 2 * BLOCK, :] = jnp.concatenate([q_ref[:, cols], g_ref[:, cols]], axis=1)
        messages[h, 2 * BLOCK :, :] = stats
    for s in range(HEADS):
        outs[s][...] = messages[me ^ s]


def fill_turned(kt, kv, j):
    kt[j] = kv[j].astype(jnp.float32).T[: LANES // 2, :].astype(jnp.bfloat16)


def fill_weight(weight, both):
    low = lax.broadcasted_iota(jnp.int32, (BLOCK, LANES), 1) < LANES // 2
    weight[:BLOCK, :] = jnp.where(low, both, jnp.zeros_like(both))
    weight[BLOCK:, :] = jnp.where(low, jnp.zeros_like(both), both)


def lists_of(rows):
    taken = [row[2 * BLOCK :, :].astype(jnp.float32)[0:1] for row in rows]
    taken += [jnp.zeros((1, LANES), jnp.float32)] * (HEADS - len(taken))
    return jnp.concatenate(taken, axis=0).astype(jnp.int32)


def run(jobs, kv, kt, total):
    head_dim = LANES // 2
    factor = math.log2(math.e) / math.sqrt(head_dim)
    steps = [(n, job[2][t : t + STEP]) for n, job in enumerate(jobs) for t in range(0, len(job[2]), STEP)]
    pairs, probabilities = {}, {}
    sums = [jnp.zeros((head_dim, BLOCK), jnp.float32) for _ in jobs]

    def score(x):
        n, spots = steps[x]
        block = jnp.concatenate([kv[i] for i in spots], axis=0)
        pairs[x] = lax.dot_general(block, jobs[n][1][...], NT, preferred_element_type=jnp.float32)

    def soften(x):
        stats = jobs[steps[x][0]][0][2 * BLOCK :, :].astype(jnp.float32)
        norm = (stats[1:2] + stats[2:3] + stats[3:4]) * math.log2(math.e)
        delta = stats[4:5] + stats[5:6] + stats[6:7]
        pair = pairs.pop(x)
        probs = jnp.exp2(pair[:, :BLOCK] * factor - norm)
        slope = (probs * (pair[:, BLOCK:] - delta)).astype(jnp.bfloat16)
        probabilities[x] = (slope, probs.astype(jnp.bfloat16))

    def spread(x):
        n, spots = steps[x]
        slope, probs = probabilities.pop(x)
        joined = jnp.concatenate([slope, probs], axis=1)
        grads = lax.dot_general(joined, jobs[n][1][...], NN, preferred_element_type=jnp.float32)
        for m, i in enumerate(spots):
            total[i] += grads[m * BLOCK : (m + 1) * BLOCK]
        flat = jnp.concatenate([kt[i] for i in spots], axis=1)
        sums[n] += lax.dot_general(flat, slope, NN, preferred_element_type=jnp.float32)

    for x in range(len(steps) + AHEAD + 1):
        if x < len(steps):
            score(x)
        if 0 <= x - AHEAD < len(steps):
            soften(x - AHEAD)
        if 0 <= x - AHEAD - 1:
            spread(x - AHEAD - 1)
    return sums


def fill_own(kv, kt, weights, s, row):
    kv[s] = row[:BLOCK, :]
    fill_turned(kt, kv, s)
    fill_weight(weights.at[s], row[BLOCK : 2 * BLOCK, :])


def fill_other(kv, kt, slots, other_ref):
    for j in range(other_ref.shape[0] // BLOCK):
        spot = HEADS * (1 + j // len(slots)) + slots[j % len(slots)]
        kv[spot] = other_ref[j * BLOCK : (j + 1) * BLOCK, :]
        fill_turned(kt, kv, spot)


def early_kernel(sizes, *rest):
    rows = rest[: len(EARLY)]
    others = rest[len(EARLY) : len(EARLY) + len(GROUPS)]
    kv, kt, weights, total, dq = rest[len(EARLY) + len(GROUPS) :]
    end = contact_plan(sizes)[0]
    lists = lists_of(rows)
    total[...] = jnp.zeros_like(total)
    dq[...] = jnp.zeros_like(dq)
    for s, row in zip(EARLY, rows):
        fill_own(kv, kt, weights, s, row)
    for slots, other_ref in zip(GROUPS, others):
        fill_other(kv, kt, slots, other_ref)
    jobs = [(rows[n], weights.at[s], [lists[n, i] for i in range(end)]) for n, s in enumerate(EARLY)]
    for s, part in zip(EARLY, run(jobs, kv, kt, total)):
        dq[s] = part


def late_kernel(*rest):
    out = rest[-1]
    for n in range(len(LATE)):
        out[n * BLOCK : (n + 1) * BLOCK, :] = rest[n][:BLOCK, :]


def first_kernel(sizes, *rest):
    rows = rest[:HEADS]
    kv, kt, weights, total, dq = rest[HEADS + 5 :]
    _, start, end, _ = contact_plan(sizes)
    lists = lists_of(rows)
    for s, row in zip(LATE, rows[len(EARLY) :]):
        fill_own(kv, kt, weights, s, row)
    jobs = [(rows[n], weights.at[s], [lists[n, i] for i in range(start, end)]) for n, s in enumerate(EARLY + LATE)]
    for s, part in zip(EARLY + LATE, run(jobs, kv, kt, total)):
        dq[s] += part


def second_kernel(sizes, *rest):
    rows = rest[:HEADS]
    other_ref, _, _, weights, _, _, kv, kt, total, dq, theirs_ref = rest[HEADS:]
    start, end, _, _ = contact_plan(sizes)
    lists = lists_of(rows)
    fill_other(kv, kt, LATE, other_ref)
    jobs = []
    for n, s in enumerate(EARLY + LATE):
        first = start if s in EARLY else 0
        jobs.append((rows[n], weights.at[s], [lists[n, i] for i in range(first, end)]))
    for s, part in zip(EARLY + LATE, run(jobs, kv, kt, total)):
        dq[s] += part
    final = final_scale()
    for j in range(theirs_ref.shape[0]):
        theirs_ref[j] = (total[HEADS + j] * final).astype(theirs_ref.dtype)


def third_kernel(sizes, *rest):
    rows = rest[:HEADS]
    kv, kt, weights, total_in, dq_in, mine_ref, dq_ref, total = rest[HEADS:]
    _, _, start, end = contact_plan(sizes)
    lists = lists_of(rows)
    for s in range(HEADS):
        total[s] = total_in[s]
    jobs = [(rows[n], weights.at[s], [lists[n, i] for i in range(start, end)]) for n, s in enumerate(EARLY + LATE)]
    for s, part in zip(EARLY + LATE, run(jobs, kv, kt, total)):
        dq_ref[s] = ((dq_in[s] + part) / math.sqrt(LANES // 2)).astype(jnp.bfloat16)
    final = final_scale()
    for s in range(HEADS):
        mine_ref[s] = total[s] * final


def final_scale():
    lane = lax.broadcasted_iota(jnp.int32, (1, LANES), 1)
    return jnp.where(lane < LANES // 2, 1.0 / math.sqrt(LANES // 2), 1.0)


def join_kernel(mine_ref, theirs_ref, dq_ref, *outs):
    for s in range(HEADS):
        both = mine_ref[s] + theirs_ref[s].astype(jnp.float32)
        outs[s][:BLOCK, :] = both.astype(jnp.bfloat16)
        outs[s][BLOCK:, :] = dq_ref[s]


def unpack_kernel(*rest):
    order = (0,) + ORDER_BACK
    parts = [rest[order.index(s)] for s in range(HEADS)]
    dq_out, dk_out, dv_out, dq_ref, dk_ref, dv_ref, messages, sems = rest[HEADS:]
    me = number()
    head_dim = LANES // 2
    for s in range(HEADS):
        messages[me ^ s] = parts[s][...]
    copies = [
        pltpu.make_async_copy(a, b, sems.at[n])
        for n, (a, b) in enumerate(((dk_ref, dk_out), (dv_ref, dv_out), (dq_ref, dq_out)))
    ]
    for target, first, copy in ((dk_ref, 0, copies[0]), (dv_ref, head_dim, copies[1])):
        for h in range(0, HEADS, 2):
            cols = slice(h * head_dim, (h + 2) * head_dim)
            pair = [messages[h + n, :BLOCK, first : first + head_dim] for n in range(2)]
            target[:, cols] = jnp.concatenate(pair, axis=1)
        copy.start()
    for h in range(0, HEADS, 2):
        cols = slice(h * head_dim, (h + 2) * head_dim)
        turned = jnp.concatenate([messages[h, BLOCK:, :], messages[h + 1, BLOCK:, :]], axis=0)
        dq_ref[:, cols] = turned.astype(jnp.float32).T.astype(jnp.bfloat16)
    copies[2].start()
    for copy in copies:
        copy.wait()


def exchange(parts, order):
    moved = {0: parts[0]}
    for s in order:
        pairs = [(j, j ^ s) for j in range(HEADS)]
        moved[s] = lax.ppermute(parts[s], ("across", "col"), pairs)
    return moved


def gather_keys(own, shares, share):
    if shares == 2:
        return lax.ppermute(own, "share", [(0, 1), (1, 0)])
    gathered = lax.all_gather(own, "share", axis=0, tiled=False)
    return gathered[jnp.arange(1, shares) ^ share].reshape(-1, LANES)


def sum_shares(theirs, shares, share):
    if shares == 2:
        return lax.ppermute(theirs, "share", [(0, 1), (1, 0)])
    full = jnp.zeros((shares, HEADS, BLOCK, LANES), jnp.float32)
    parts = theirs.reshape(shares - 1, HEADS, BLOCK, LANES).astype(jnp.float32)
    full = full.at[jnp.arange(1, shares) ^ share].set(parts)
    return lax.psum_scatter(full, "share", scatter_dimension=0, tiled=False)


def call(kernel, outs, in_specs, scratch=(), tiles=0, aliases=None, out_space=VMEM):
    flops = tiles * 10 * BLOCK * BLOCK * (LANES // 2)
    cost = pl.CostEstimate(flops=flops, bytes_accessed=tiles << 14, transcendentals=tiles * BLOCK * BLOCK)
    return pl.pallas_call(
        kernel,
        out_shape=[jax.ShapeDtypeStruct(shape, dtype) for shape, dtype in outs],
        in_specs=in_specs,
        out_specs=[out_space] * len(outs),
        scratch_shapes=list(scratch),
        cost_estimate=cost,
        input_output_aliases=aliases or {},
        compiler_params=pltpu.CompilerParams(vmem_limit_bytes=48 * 1024 * 1024),
    )


def body(queries, keys, values, outputs, out_grad, log_norm, contacts):
    bf16, f32 = jnp.bfloat16, jnp.float32
    width = queries.shape[1]
    columns = lax.axis_size("col")
    across = lax.axis_size("across")
    shares = lax.axis_size("share")
    contact_count = contacts.shape[1]
    sizes = (shares, across, columns, contact_count)
    count = shares * HEADS
    half = LANES // 2
    share = lax.axis_index("share")
    length = 2 * BLOCK + STATS
    loaded = [
        pltpu.with_memory_space_constraint(a, pltpu.HBM)
        for a in (contacts, queries, keys, values, outputs, out_grad, log_norm)
    ]
    packed = call(
        lambda *refs: pack_kernel(sizes, *refs),
        [((length, LANES), bf16)] * HEADS,
        [HBM] * 7,
        [
            pltpu.VMEM((HEADS, length, LANES), bf16),
            pltpu.SMEM(contacts.shape, jnp.int32),
            *[pltpu.VMEM(a.shape, a.dtype) for a in loaded[1:]],
            pltpu.SemaphoreType.DMA((7,)),
        ],
    )(*loaded)
    moved = exchange(packed, ORDER_OUT)
    early, late = [moved[s] for s in EARLY], [moved[s] for s in LATE]
    plan = contact_plan(sizes)
    held = [
        ((count, BLOCK, LANES), bf16),
        ((count, half, LANES), bf16),
        ((HEADS, 2 * BLOCK, LANES), bf16),
        ((count, BLOCK, LANES), f32),
        ((HEADS, half, BLOCK), f32),
    ]
    others = [
        gather_keys(jnp.concatenate([moved[s][:BLOCK] for s in slots], axis=0), shares, share) for slots in GROUPS
    ]
    kv, kt, weights, total, dq = call(
        lambda *refs: early_kernel(sizes, *refs),
        held,
        [VMEM] * (len(EARLY) + len(GROUPS)),
    )(*early, *others)
    own = call(late_kernel, [((len(LATE) * BLOCK, LANES), bf16)], [VMEM] * (len(LATE) + 1))(*late, dq)[0]
    other = gather_keys(own, shares, share)
    kv, kt, weights, total, dq = call(
        lambda *refs: first_kernel(sizes, *refs),
        held,
        [VMEM] * (HEADS + 5),
        tiles=HEADS * (plan[2] - plan[1]) + 12,
        aliases={HEADS + n: n for n in range(5)},
    )(*early, *late, kv, kt, weights, total, dq)
    kv, kt, total, dq, theirs = call(
        lambda *refs: second_kernel(sizes, *refs),
        [held[0], held[1], held[3], held[4], ((count - HEADS, BLOCK, LANES), bf16)],
        [VMEM] * (HEADS + 6),
        tiles=HEADS * (plan[1] - plan[0]) + len(LATE) * plan[0],
        aliases={HEADS + 1: 0, HEADS + 2: 1, HEADS + 4: 2, HEADS + 5: 3},
    )(*early, *late, other, kv, kt, weights, total, dq)
    arrived = sum_shares(theirs, shares, share)
    mine, dq = call(
        lambda *refs: third_kernel(sizes, *refs),
        [((HEADS, BLOCK, LANES), f32), ((HEADS, half, BLOCK), bf16)],
        [VMEM] * (HEADS + 5),
        [pltpu.VMEM((HEADS, BLOCK, LANES), f32)],
        tiles=HEADS * (plan[3] - plan[2]) + 1,
    )(*early, *late, kv, kt, weights, total, dq)
    joined = call(
        join_kernel,
        [((BLOCK + half, LANES), bf16)] * HEADS,
        [VMEM] * 3,
    )(mine, arrived, dq)
    back = exchange(joined, ORDER_BACK)
    return call(
        unpack_kernel,
        [((BLOCK, width), bf16)] * 3,
        [VMEM] * HEADS,
        [pltpu.VMEM((BLOCK, width), bf16)] * 3
        + [pltpu.VMEM((HEADS, BLOCK + half, LANES), bf16), pltpu.SemaphoreType.DMA((3,))],
        out_space=HBM,
    )(*[back[s] for s in (0,) + ORDER_BACK])


def solution(mesh):
    groups, rows, columns = (mesh.shape[a] for a in ("groups", "row", "col"))
    across = HEADS // columns
    shape = (groups, across, rows // across, columns)
    split = Mesh(mesh.devices.reshape(shape), ("groups", "across", "share", "col"))
    query_side = ("groups", "across", "share", "col")
    key_side = ("groups", "col", "across", "share")
    in_specs = (
        P(query_side, None),
        P(key_side, None),
        P(key_side, None),
        P(query_side, None),
        P(query_side, None),
        P(None, query_side),
        P(("groups", "across", "share"), None),
    )
    out_specs = (P(query_side, None), P(key_side, None), P(key_side, None))
    return jax.shard_map(body, mesh=split, in_specs=in_specs, out_specs=out_specs, check_vma=False)
```

```python
import math

import jax
import jax.numpy as jnp
from jax import lax
from jax.experimental import pallas as pl
from jax.experimental.pallas import tpu as pltpu
from jax.sharding import Mesh
from jax.sharding import PartitionSpec as P

BLOCK = 128
LANES = 128
HEADS = 8
STATS = 16
PIECE = 32
STEP = 2
AHEAD = 3
NT = (((1,), (1,)), ((), ()))
NN = (((1,), (0,)), ((), ()))
VMEM = pl.BlockSpec(memory_space=pltpu.VMEM)
SMEM = pl.BlockSpec(memory_space=pltpu.SMEM)
HBM = pl.BlockSpec(memory_space=pltpu.HBM)
ORDER_OUT = (4, 2, 7, 5, 1, 6, 3)
ORDER_BACK = (3, 2, 6, 7, 5, 4, 1)
LATE = (6, 3)
GROUPS = ((0, 4), (2, 7), (5, 1))
EARLY = sum(GROUPS, ())


def contact_plan(sizes):
    shares, contact_count = sizes[0], sizes[3]
    home = max(0, contact_count - (shares - 1) * HEADS)
    late = len(LATE) * (shares - 1 if home >= len(LATE) else shares)
    away = contact_count - home
    return max(0, away - late), away, away + home // 2, contact_count


def number():
    return lax.axis_index("across") * lax.axis_size("col") + lax.axis_index("col")


def split_three(x):
    hi = x.astype(jnp.bfloat16).astype(jnp.float32)
    rest = x - hi
    mid = rest.astype(jnp.bfloat16).astype(jnp.float32)
    return hi, mid, rest - mid


def listed_contacts(contacts_ref, column, share, sizes):
    shares, across, columns, contact_count = sizes
    away_count = contact_plan(sizes)[1]
    home = contact_count - away_count
    target = lax.broadcasted_iota(jnp.int32, (HEADS, LANES), 0)
    lane = lax.broadcasted_iota(jnp.int32, (HEADS, LANES), 1)
    spots, ranks = [], []
    for i in range(contact_count):
        block = contacts_ref[column, i]
        col = block // (across * shares)
        rem = block - col * (across * shares)
        row = rem // shares
        away = (rem - row * shares) ^ share
        slot = target ^ (row * columns + col)
        late = sum((slot == s).astype(jnp.int32) for s in LATE)
        spots.append(away * HEADS + slot)
        ranks.append(jnp.where(away == 0, -late, 2 + late) * contact_count + i)
    listed = jnp.zeros((HEADS, LANES), jnp.int32)
    for i in range(contact_count):
        rank = sum((ranks[j] < ranks[i]).astype(jnp.int32) for j in range(contact_count) if j != i)
        place = jnp.where(rank < home, rank + away_count, rank - home)
        listed = jnp.where(lane == place, spots[i], listed)
    return listed


def pack_kernel(sizes, contacts_hbm, *rest):
    sources, outs = rest[:6], rest[6 : 6 + HEADS]
    messages, contacts_ref, q_ref, k_ref, v_ref, o_ref, g_ref, norm_ref, sems = rest[6 + HEADS :]
    targets = (q_ref, k_ref, v_ref, o_ref, g_ref, norm_ref)
    pairs = ((contacts_hbm, contacts_ref),) + tuple(zip(sources, targets))

    def wait(*which):
        for i in which:
            pltpu.make_async_copy(*pairs[i], sems.at[i]).wait()

    for i in (0, 5, 4, 6, 1, 2, 3):
        a, b = pairs[i]
        size = PIECE if a.shape[0] == BLOCK else a.shape[0]
        for r in range(0, a.shape[0], size):
            pltpu.make_async_copy(a.at[pl.ds(r, size)], b.at[pl.ds(r, size)], sems.at[i]).start()
    width = q_ref.shape[1]
    head_dim = width // HEADS
    me, column, share = number(), lax.axis_index("col"), lax.axis_index("share")
    wait(0)
    listed = listed_contacts(contacts_ref, column, share, sizes).astype(jnp.float32)
    wait(5, 4, 6)
    products = g_ref[...].astype(jnp.float32) * o_ref[...].astype(jnp.float32)
    hi = products.astype(jnp.bfloat16)
    lo = (products - hi.astype(jnp.float32)).astype(jnp.bfloat16)
    owner = lax.broadcasted_iota(jnp.int32, (HEADS, width), 1) // head_dim
    picks = (owner == lax.broadcasted_iota(jnp.int32, (HEADS, width), 0)).astype(jnp.bfloat16)
    delta = lax.dot_general(picks, hi, NT, preferred_element_type=jnp.float32)
    delta += lax.dot_general(picks, lo, NT, preferred_element_type=jnp.float32)
    norm_parts = split_three(norm_ref[...])
    delta_parts = split_three(delta)
    wait(1, 2, 3)
    blank = jnp.zeros((STATS - 7, LANES), jnp.float32)
    for h in range(HEADS):
        cols = slice(h * head_dim, (h + 1) * head_dim)
        rows = [part[h : h + 1] for part in (listed,) + norm_parts + delta_parts]
        stats = jnp.concatenate(rows + [blank], axis=0).astype(jnp.bfloat16)
        messages[h, :BLOCK, :] = jnp.concatenate([k_ref[:, cols], v_ref[:, cols]], axis=1)
        messages[h, BLOCK : 2 * BLOCK, :] = jnp.concatenate([q_ref[:, cols], g_ref[:, cols]], axis=1)
        messages[h, 2 * BLOCK :, :] = stats
    for s in range(HEADS):
        outs[s][...] = messages[me ^ s]


def fill_turned(kt, kv, j):
    kt[j] = kv[j].astype(jnp.float32).T[: LANES // 2, :].astype(jnp.bfloat16)


def fill_weight(weight, both):
    low = lax.broadcasted_iota(jnp.int32, (BLOCK, LANES), 1) < LANES // 2
    weight[:BLOCK, :] = jnp.where(low, both, jnp.zeros_like(both))
    weight[BLOCK:, :] = jnp.where(low, jnp.zeros_like(both), both)


def lists_of(rows):
    taken = [row[2 * BLOCK :, :].astype(jnp.float32)[0:1] for row in rows]
    taken += [jnp.zeros((1, LANES), jnp.float32)] * (HEADS - len(taken))
    return jnp.concatenate(taken, axis=0).astype(jnp.int32)


def run(jobs, kv, kt, total):
    head_dim = LANES // 2
    factor = math.log2(math.e) / math.sqrt(head_dim)
    steps = [(n, job[2][t : t + STEP]) for n, job in enumerate(jobs) for t in range(0, len(job[2]), STEP)]
    pairs, probabilities = {}, {}
    sums = [jnp.zeros((head_dim, BLOCK), jnp.float32) for _ in jobs]

    def score(x):
        n, spots = steps[x]
        block = jnp.concatenate([kv[i] for i in spots], axis=0)
        pairs[x] = lax.dot_general(block, jobs[n][1][...], NT, preferred_element_type=jnp.float32)

    def soften(x):
        stats = jobs[steps[x][0]][0][2 * BLOCK :, :].astype(jnp.float32)
        norm = (stats[1:2] + stats[2:3] + stats[3:4]) * math.log2(math.e)
        delta = stats[4:5] + stats[5:6] + stats[6:7]
        pair = pairs.pop(x)
        probs = jnp.exp2(pair[:, :BLOCK] * factor - norm)
        slope = (probs * (pair[:, BLOCK:] - delta)).astype(jnp.bfloat16)
        probabilities[x] = (slope, probs.astype(jnp.bfloat16))

    def spread(x):
        n, spots = steps[x]
        slope, probs = probabilities.pop(x)
        joined = jnp.concatenate([slope, probs], axis=1)
        grads = lax.dot_general(joined, jobs[n][1][...], NN, preferred_element_type=jnp.float32)
        for m, i in enumerate(spots):
            total[i] += grads[m * BLOCK : (m + 1) * BLOCK]
        flat = jnp.concatenate([kt[i] for i in spots], axis=1)
        sums[n] += lax.dot_general(flat, slope, NN, preferred_element_type=jnp.float32)

    for x in range(len(steps) + AHEAD + 1):
        if x < len(steps):
            score(x)
        if 0 <= x - AHEAD < len(steps):
            soften(x - AHEAD)
        if 0 <= x - AHEAD - 1:
            spread(x - AHEAD - 1)
    return sums


def fill_own(kv, kt, weights, s, row):
    kv[s] = row[:BLOCK, :]
    fill_turned(kt, kv, s)
    fill_weight(weights.at[s], row[BLOCK : 2 * BLOCK, :])


def fill_other(kv, kt, slots, other_ref):
    for j in range(other_ref.shape[0] // BLOCK):
        spot = HEADS * (1 + j // len(slots)) + slots[j % len(slots)]
        kv[spot] = other_ref[j * BLOCK : (j + 1) * BLOCK, :]
        fill_turned(kt, kv, spot)


def early_kernel(sizes, *rest):
    rows = rest[: len(EARLY)]
    others = rest[len(EARLY) : len(EARLY) + len(GROUPS)]
    kv, kt, weights, total, dq = rest[len(EARLY) + len(GROUPS) :]
    end = contact_plan(sizes)[0]
    lists = lists_of(rows)
    total[...] = jnp.zeros_like(total)
    dq[...] = jnp.zeros_like(dq)
    for s, row in zip(EARLY, rows):
        fill_own(kv, kt, weights, s, row)
    for slots, other_ref in zip(GROUPS, others):
        fill_other(kv, kt, slots, other_ref)
    jobs = [(rows[n], weights.at[s], [lists[n, i] for i in range(end)]) for n, s in enumerate(EARLY)]
    for s, part in zip(EARLY, run(jobs, kv, kt, total)):
        dq[s] = part


def late_kernel(*rest):
    out = rest[-1]
    for n in range(len(LATE)):
        out[n * BLOCK : (n + 1) * BLOCK, :] = rest[n][:BLOCK, :]


def first_kernel(sizes, *rest):
    rows = rest[:HEADS]
    kv, kt, weights, total, dq = rest[HEADS + 5 :]
    _, start, end, _ = contact_plan(sizes)
    lists = lists_of(rows)
    for s, row in zip(LATE, rows[len(EARLY) :]):
        fill_own(kv, kt, weights, s, row)
    jobs = [(rows[n], weights.at[s], [lists[n, i] for i in range(start, end)]) for n, s in enumerate(EARLY + LATE)]
    for s, part in zip(EARLY + LATE, run(jobs, kv, kt, total)):
        dq[s] += part


def second_kernel(sizes, *rest):
    rows = rest[:HEADS]
    other_ref, _, _, weights, _, _, kv, kt, total, dq, theirs_ref = rest[HEADS:]
    start, end, _, _ = contact_plan(sizes)
    lists = lists_of(rows)
    fill_other(kv, kt, LATE, other_ref)
    jobs = []
    for n, s in enumerate(EARLY + LATE):
        first = start if s in EARLY else 0
        jobs.append((rows[n], weights.at[s], [lists[n, i] for i in range(first, end)]))
    for s, part in zip(EARLY + LATE, run(jobs, kv, kt, total)):
        dq[s] += part
    final = final_scale()
    for j in range(theirs_ref.shape[0]):
        theirs_ref[j] = (total[HEADS + j] * final).astype(theirs_ref.dtype)


def third_kernel(sizes, *rest):
    rows = rest[:HEADS]
    kv, kt, weights, total_in, dq_in, mine_ref, dq_ref, total = rest[HEADS:]
    _, _, start, end = contact_plan(sizes)
    lists = lists_of(rows)
    for s in range(HEADS):
        total[s] = total_in[s]
    jobs = [(rows[n], weights.at[s], [lists[n, i] for i in range(start, end)]) for n, s in enumerate(EARLY + LATE)]
    for s, part in zip(EARLY + LATE, run(jobs, kv, kt, total)):
        dq_ref[s] = ((dq_in[s] + part) / math.sqrt(LANES // 2)).astype(jnp.bfloat16)
    final = final_scale()
    for s in range(HEADS):
        mine_ref[s] = total[s] * final


def final_scale():
    lane = lax.broadcasted_iota(jnp.int32, (1, LANES), 1)
    return jnp.where(lane < LANES // 2, 1.0 / math.sqrt(LANES // 2), 1.0)


def join_kernel(mine_ref, theirs_ref, dq_ref, *outs):
    for s in range(HEADS):
        both = mine_ref[s] + theirs_ref[s].astype(jnp.float32)
        outs[s][:BLOCK, :] = both.astype(jnp.bfloat16)
        outs[s][BLOCK:, :] = dq_ref[s]


def unpack_kernel(*rest):
    order = (0,) + ORDER_BACK
    parts = [rest[order.index(s)] for s in range(HEADS)]
    dq_out, dk_out, dv_out, dq_ref, dk_ref, dv_ref, messages, sems = rest[HEADS:]
    me = number()
    head_dim = LANES // 2
    for s in range(HEADS):
        messages[me ^ s] = parts[s][...]
    copies = [
        pltpu.make_async_copy(a, b, sems.at[n])
        for n, (a, b) in enumerate(((dk_ref, dk_out), (dv_ref, dv_out), (dq_ref, dq_out)))
    ]
    for target, first, copy in ((dk_ref, 0, copies[0]), (dv_ref, head_dim, copies[1])):
        for h in range(0, HEADS, 2):
            cols = slice(h * head_dim, (h + 2) * head_dim)
            pair = [messages[h + n, :BLOCK, first : first + head_dim] for n in range(2)]
            target[:, cols] = jnp.concatenate(pair, axis=1)
        copy.start()
    for h in range(0, HEADS, 2):
        cols = slice(h * head_dim, (h + 2) * head_dim)
        turned = jnp.concatenate([messages[h, BLOCK:, :], messages[h + 1, BLOCK:, :]], axis=0)
        dq_ref[:, cols] = turned.astype(jnp.float32).T.astype(jnp.bfloat16)
    copies[2].start()
    for copy in copies:
        copy.wait()


def exchange(parts, order):
    moved = {0: parts[0]}
    for s in order:
        pairs = [(j, j ^ s) for j in range(HEADS)]
        moved[s] = lax.ppermute(parts[s], ("across", "col"), pairs)
    return moved


def gather_keys(own, shares, share):
    if shares == 2:
        return lax.ppermute(own, "share", [(0, 1), (1, 0)])
    gathered = lax.all_gather(own, "share", axis=0, tiled=False)
    return gathered[jnp.arange(1, shares) ^ share].reshape(-1, LANES)


def sum_shares(theirs, shares, share):
    if shares == 2:
        return lax.ppermute(theirs, "share", [(0, 1), (1, 0)])
    full = jnp.zeros((shares, HEADS, BLOCK, LANES), jnp.float32)
    parts = theirs.reshape(shares - 1, HEADS, BLOCK, LANES).astype(jnp.float32)
    full = full.at[jnp.arange(1, shares) ^ share].set(parts)
    return lax.psum_scatter(full, "share", scatter_dimension=0, tiled=False)


def call(kernel, outs, in_specs, scratch=(), tiles=0, aliases=None, out_space=VMEM):
    flops = tiles * 10 * BLOCK * BLOCK * (LANES // 2)
    cost = pl.CostEstimate(flops=flops, bytes_accessed=tiles << 14, transcendentals=tiles * BLOCK * BLOCK)
    return pl.pallas_call(
        kernel,
        out_shape=[jax.ShapeDtypeStruct(shape, dtype) for shape, dtype in outs],
        in_specs=in_specs,
        out_specs=[out_space] * len(outs),
        scratch_shapes=list(scratch),
        cost_estimate=cost,
        input_output_aliases=aliases or {},
        compiler_params=pltpu.CompilerParams(vmem_limit_bytes=48 * 1024 * 1024),
    )


def body(queries, keys, values, outputs, out_grad, log_norm, contacts):
    bf16, f32 = jnp.bfloat16, jnp.float32
    width = queries.shape[1]
    columns = lax.axis_size("col")
    across = lax.axis_size("across")
    shares = lax.axis_size("share")
    contact_count = contacts.shape[1]
    sizes = (shares, across, columns, contact_count)
    count = shares * HEADS
    half = LANES // 2
    share = lax.axis_index("share")
    length = 2 * BLOCK + STATS
    loaded = [
        pltpu.with_memory_space_constraint(a, pltpu.HBM)
        for a in (contacts, queries, keys, values, outputs, out_grad, log_norm)
    ]
    packed = call(
        lambda *refs: pack_kernel(sizes, *refs),
        [((length, LANES), bf16)] * HEADS,
        [HBM] * 7,
        [
            pltpu.VMEM((HEADS, length, LANES), bf16),
            pltpu.SMEM(contacts.shape, jnp.int32),
            *[pltpu.VMEM(a.shape, a.dtype) for a in loaded[1:]],
            pltpu.SemaphoreType.DMA((7,)),
        ],
    )(*loaded)
    moved = exchange(packed, ORDER_OUT)
    early, late = [moved[s] for s in EARLY], [moved[s] for s in LATE]
    plan = contact_plan(sizes)
    held = [
        ((count, BLOCK, LANES), bf16),
        ((count, half, LANES), bf16),
        ((HEADS, 2 * BLOCK, LANES), bf16),
        ((count, BLOCK, LANES), f32),
        ((HEADS, half, BLOCK), f32),
    ]
    others = [
        gather_keys(jnp.concatenate([moved[s][:BLOCK] for s in slots], axis=0), shares, share) for slots in GROUPS
    ]
    kv, kt, weights, total, dq = call(
        lambda *refs: early_kernel(sizes, *refs),
        held,
        [VMEM] * (len(EARLY) + len(GROUPS)),
    )(*early, *others)
    own = call(late_kernel, [((len(LATE) * BLOCK, LANES), bf16)], [VMEM] * (len(LATE) + 1))(*late, dq)[0]
    other = gather_keys(own, shares, share)
    kv, kt, weights, total, dq = call(
        lambda *refs: first_kernel(sizes, *refs),
        held,
        [VMEM] * (HEADS + 5),
        tiles=HEADS * (plan[2] - plan[1]) + 12,
        aliases={HEADS + n: n for n in range(5)},
    )(*early, *late, kv, kt, weights, total, dq)
    kv, kt, total, dq, theirs = call(
        lambda *refs: second_kernel(sizes, *refs),
        [held[0], held[1], held[3], held[4], ((count - HEADS, BLOCK, LANES), bf16)],
        [VMEM] * (HEADS + 6),
        tiles=HEADS * (plan[1] - plan[0]) + len(LATE) * plan[0],
        aliases={HEADS + 1: 0, HEADS + 2: 1, HEADS + 4: 2, HEADS + 5: 3},
    )(*early, *late, other, kv, kt, weights, total, dq)
    arrived = sum_shares(theirs, shares, share)
    mine, dq = call(
        lambda *refs: third_kernel(sizes, *refs),
        [((HEADS, BLOCK, LANES), f32), ((HEADS, half, BLOCK), bf16)],
        [VMEM] * (HEADS + 5),
        [pltpu.VMEM((HEADS, BLOCK, LANES), f32)],
        tiles=HEADS * (plan[3] - plan[2]) + 1,
    )(*early, *late, kv, kt, weights, total, dq)
    joined = call(
        join_kernel,
        [((BLOCK + half, LANES), bf16)] * HEADS,
        [VMEM] * 3,
    )(mine, arrived, dq)
    back = exchange(joined, ORDER_BACK)
    return call(
        unpack_kernel,
        [((BLOCK, width), bf16)] * 3,
        [VMEM] * HEADS,
        [pltpu.VMEM((BLOCK, width), bf16)] * 3
        + [pltpu.VMEM((HEADS, BLOCK + half, LANES), bf16), pltpu.SemaphoreType.DMA((3,))],
        out_space=HBM,
    )(*[back[s] for s in (0,) + ORDER_BACK])


def solution(mesh):
    groups, rows, columns = (mesh.shape[a] for a in ("groups", "row", "col"))
    across = HEADS // columns
    shape = (groups, across, rows // across, columns)
    split = Mesh(mesh.devices.reshape(shape), ("groups", "across", "share", "col"))
    query_side = ("groups", "across", "share", "col")
    key_side = ("groups", "col", "across", "share")
    in_specs = (
        P(query_side, None),
        P(key_side, None),
        P(key_side, None),
        P(query_side, None),
        P(query_side, None),
        P(None, query_side),
        P(("groups", "across", "share"), None),
    )
    out_specs = (P(query_side, None), P(key_side, None), P(key_side, None))
    return jax.shard_map(body, mesh=split, in_specs=in_specs, out_specs=out_specs, check_vma=False)
```

```python
import math

import jax
import jax.numpy as jnp
from jax import lax
from jax.experimental import pallas as pl
from jax.experimental.pallas import tpu as pltpu
from jax.sharding import Mesh
from jax.sharding import PartitionSpec as P

BLOCK = 128
LANES = 128
HEADS = 8
STATS = 16
PIECE = 32
STEP = 2
AHEAD = 3
NT = (((1,), (1,)), ((), ()))
NN = (((1,), (0,)), ((), ()))
VMEM = pl.BlockSpec(memory_space=pltpu.VMEM)
SMEM = pl.BlockSpec(memory_space=pltpu.SMEM)
HBM = pl.BlockSpec(memory_space=pltpu.HBM)
ORDER_OUT = (4, 2, 7, 5, 1, 6, 3)
ORDER_BACK = (3, 2, 6, 7, 5, 4, 1)
LATE = (6, 3)
GROUPS = ((0, 4), (2, 7), (5, 1))
EARLY = sum(GROUPS, ())


def contact_plan(sizes):
    shares, contact_count = sizes[0], sizes[3]
    home = max(0, contact_count - (shares - 1) * HEADS)
    late = len(LATE) * (shares - 1 if home >= len(LATE) else shares)
    away = contact_count - home
    return max(0, away - late), away, away + home // 4, contact_count


def number():
    return lax.axis_index("across") * lax.axis_size("col") + lax.axis_index("col")


def split_three(x):
    hi = x.astype(jnp.bfloat16).astype(jnp.float32)
    rest = x - hi
    mid = rest.astype(jnp.bfloat16).astype(jnp.float32)
    return hi, mid, rest - mid


def listed_contacts(contacts_ref, column, share, sizes):
    shares, across, columns, contact_count = sizes
    away_count = contact_plan(sizes)[1]
    home = contact_count - away_count
    target = lax.broadcasted_iota(jnp.int32, (HEADS, LANES), 0)
    lane = lax.broadcasted_iota(jnp.int32, (HEADS, LANES), 1)
    spots, ranks = [], []
    for i in range(contact_count):
        block = contacts_ref[column, i]
        col = block // (across * shares)
        rem = block - col * (across * shares)
        row = rem // shares
        away = (rem - row * shares) ^ share
        slot = target ^ (row * columns + col)
        late = sum((slot == s).astype(jnp.int32) for s in LATE)
        spots.append(away * HEADS + slot)
        ranks.append(jnp.where(away == 0, -late, 2 + late) * contact_count + i)
    listed = jnp.zeros((HEADS, LANES), jnp.int32)
    for i in range(contact_count):
        rank = sum((ranks[j] < ranks[i]).astype(jnp.int32) for j in range(contact_count) if j != i)
        place = jnp.where(rank < home, rank + away_count, rank - home)
        listed = jnp.where(lane == place, spots[i], listed)
    return listed


def pack_kernel(sizes, contacts_hbm, *rest):
    sources, outs = rest[:6], rest[6 : 6 + HEADS]
    messages, contacts_ref, q_ref, k_ref, v_ref, o_ref, g_ref, norm_ref, sems = rest[6 + HEADS :]
    targets = (q_ref, k_ref, v_ref, o_ref, g_ref, norm_ref)
    pairs = ((contacts_hbm, contacts_ref),) + tuple(zip(sources, targets))

    def wait(*which):
        for i in which:
            pltpu.make_async_copy(*pairs[i], sems.at[i]).wait()

    for i in (0, 5, 4, 6, 1, 2, 3):
        a, b = pairs[i]
        size = PIECE if a.shape[0] == BLOCK else a.shape[0]
        for r in range(0, a.shape[0], size):
            pltpu.make_async_copy(a.at[pl.ds(r, size)], b.at[pl.ds(r, size)], sems.at[i]).start()
    width = q_ref.shape[1]
    head_dim = width // HEADS
    me, column, share = number(), lax.axis_index("col"), lax.axis_index("share")
    wait(0)
    listed = listed_contacts(contacts_ref, column, share, sizes).astype(jnp.float32)
    wait(5, 4, 6)
    products = g_ref[...].astype(jnp.float32) * o_ref[...].astype(jnp.float32)
    hi = products.astype(jnp.bfloat16)
    lo = (products - hi.astype(jnp.float32)).astype(jnp.bfloat16)
    owner = lax.broadcasted_iota(jnp.int32, (HEADS, width), 1) // head_dim
    picks = (owner == lax.broadcasted_iota(jnp.int32, (HEADS, width), 0)).astype(jnp.bfloat16)
    delta = lax.dot_general(picks, hi, NT, preferred_element_type=jnp.float32)
    delta += lax.dot_general(picks, lo, NT, preferred_element_type=jnp.float32)
    norm_parts = split_three(norm_ref[...])
    delta_parts = split_three(delta)
    wait(1, 2, 3)
    blank = jnp.zeros((STATS - 7, LANES), jnp.float32)
    for h in range(HEADS):
        cols = slice(h * head_dim, (h + 1) * head_dim)
        rows = [part[h : h + 1] for part in (listed,) + norm_parts + delta_parts]
        stats = jnp.concatenate(rows + [blank], axis=0).astype(jnp.bfloat16)
        messages[h, :BLOCK, :] = jnp.concatenate([k_ref[:, cols], v_ref[:, cols]], axis=1)
        messages[h, BLOCK : 2 * BLOCK, :] = jnp.concatenate([q_ref[:, cols], g_ref[:, cols]], axis=1)
        messages[h, 2 * BLOCK :, :] = stats
    for s in range(HEADS):
        outs[s][...] = messages[me ^ s]


def fill_turned(kt, kv, j):
    kt[j] = kv[j].astype(jnp.float32).T[: LANES // 2, :].astype(jnp.bfloat16)


def fill_weight(weight, both):
    low = lax.broadcasted_iota(jnp.int32, (BLOCK, LANES), 1) < LANES // 2
    weight[:BLOCK, :] = jnp.where(low, both, jnp.zeros_like(both))
    weight[BLOCK:, :] = jnp.where(low, jnp.zeros_like(both), both)


def lists_of(rows):
    taken = [row[2 * BLOCK :, :].astype(jnp.float32)[0:1] for row in rows]
    taken += [jnp.zeros((1, LANES), jnp.float32)] * (HEADS - len(taken))
    return jnp.concatenate(taken, axis=0).astype(jnp.int32)


def run(jobs, kv, kt, total):
    head_dim = LANES // 2
    factor = math.log2(math.e) / math.sqrt(head_dim)
    steps = [(n, job[2][t : t + STEP]) for n, job in enumerate(jobs) for t in range(0, len(job[2]), STEP)]
    pairs, probabilities = {}, {}
    sums = [jnp.zeros((head_dim, BLOCK), jnp.float32) for _ in jobs]

    def score(x):
        n, spots = steps[x]
        block = jnp.concatenate([kv[i] for i in spots], axis=0)
        pairs[x] = lax.dot_general(block, jobs[n][1][...], NT, preferred_element_type=jnp.float32)

    def soften(x):
        stats = jobs[steps[x][0]][0][2 * BLOCK :, :].astype(jnp.float32)
        norm = (stats[1:2] + stats[2:3] + stats[3:4]) * math.log2(math.e)
        delta = stats[4:5] + stats[5:6] + stats[6:7]
        pair = pairs.pop(x)
        probs = jnp.exp2(pair[:, :BLOCK] * factor - norm)
        slope = (probs * (pair[:, BLOCK:] - delta)).astype(jnp.bfloat16)
        probabilities[x] = (slope, probs.astype(jnp.bfloat16))

    def spread(x):
        n, spots = steps[x]
        slope, probs = probabilities.pop(x)
        joined = jnp.concatenate([slope, probs], axis=1)
        grads = lax.dot_general(joined, jobs[n][1][...], NN, preferred_element_type=jnp.float32)
        for m, i in enumerate(spots):
            total[i] += grads[m * BLOCK : (m + 1) * BLOCK]
        flat = jnp.concatenate([kt[i] for i in spots], axis=1)
        sums[n] += lax.dot_general(flat, slope, NN, preferred_element_type=jnp.float32)

    for x in range(len(steps) + AHEAD + 1):
        if x < len(steps):
            score(x)
        if 0 <= x - AHEAD < len(steps):
            soften(x - AHEAD)
        if 0 <= x - AHEAD - 1:
            spread(x - AHEAD - 1)
    return sums


def fill_own(kv, kt, weights, s, row):
    kv[s] = row[:BLOCK, :]
    fill_turned(kt, kv, s)
    fill_weight(weights.at[s], row[BLOCK : 2 * BLOCK, :])


def fill_other(kv, kt, slots, other_ref):
    for j in range(other_ref.shape[0] // BLOCK):
        spot = HEADS * (1 + j // len(slots)) + slots[j % len(slots)]
        kv[spot] = other_ref[j * BLOCK : (j + 1) * BLOCK, :]
        fill_turned(kt, kv, spot)


def early_kernel(sizes, *rest):
    rows = rest[: len(EARLY)]
    others = rest[len(EARLY) : len(EARLY) + len(GROUPS)]
    kv, kt, weights, total, dq = rest[len(EARLY) + len(GROUPS) :]
    end = contact_plan(sizes)[0]
    lists = lists_of(rows)
    total[...] = jnp.zeros_like(total)
    dq[...] = jnp.zeros_like(dq)
    for s, row in zip(EARLY, rows):
        fill_own(kv, kt, weights, s, row)
    for slots, other_ref in zip(GROUPS, others):
        fill_other(kv, kt, slots, other_ref)
    jobs = [(rows[n], weights.at[s], [lists[n, i] for i in range(end)]) for n, s in enumerate(EARLY)]
    for s, part in zip(EARLY, run(jobs, kv, kt, total)):
        dq[s] = part


def late_kernel(*rest):
    out = rest[-1]
    for n in range(len(LATE)):
        out[n * BLOCK : (n + 1) * BLOCK, :] = rest[n][:BLOCK, :]


def first_kernel(sizes, *rest):
    rows = rest[:HEADS]
    kv, kt, weights, total, dq = rest[HEADS + 5 :]
    first, start, end, _ = contact_plan(sizes)
    lists = lists_of(rows)
    for s, row in zip(LATE, rows[len(EARLY) :]):
        fill_own(kv, kt, weights, s, row)
    jobs = []
    for n, s in enumerate(EARLY + LATE):
        places = list(range(start, end)) + list(range(first if s in LATE else 0))
        jobs.append((rows[n], weights.at[s], [lists[n, i] for i in places]))
    for s, part in zip(EARLY + LATE, run(jobs, kv, kt, total)):
        dq[s] += part


def second_kernel(sizes, *rest):
    rows = rest[:HEADS]
    other_ref, _, _, weights, _, _, kv, kt, total, dq, theirs_ref = rest[HEADS:]
    start, end, _, _ = contact_plan(sizes)
    lists = lists_of(rows)
    fill_other(kv, kt, LATE, other_ref)
    jobs = [(rows[n], weights.at[s], [lists[n, i] for i in range(start, end)]) for n, s in enumerate(EARLY + LATE)]
    for s, part in zip(EARLY + LATE, run(jobs, kv, kt, total)):
        dq[s] += part
    final = final_scale()
    for j in range(theirs_ref.shape[0]):
        theirs_ref[j] = (total[HEADS + j] * final).astype(theirs_ref.dtype)


def third_kernel(sizes, *rest):
    rows = rest[:HEADS]
    kv, kt, weights, total_in, dq_in, mine_ref, dq_ref, total = rest[HEADS:]
    _, _, start, end = contact_plan(sizes)
    lists = lists_of(rows)
    for s in range(HEADS):
        total[s] = total_in[s]
    jobs = [(rows[n], weights.at[s], [lists[n, i] for i in range(start, end)]) for n, s in enumerate(EARLY + LATE)]
    for s, part in zip(EARLY + LATE, run(jobs, kv, kt, total)):
        dq_ref[s] = ((dq_in[s] + part) / math.sqrt(LANES // 2)).astype(jnp.bfloat16)
    final = final_scale()
    for s in range(HEADS):
        mine_ref[s] = total[s] * final


def final_scale():
    lane = lax.broadcasted_iota(jnp.int32, (1, LANES), 1)
    return jnp.where(lane < LANES // 2, 1.0 / math.sqrt(LANES // 2), 1.0)


def join_kernel(mine_ref, theirs_ref, dq_ref, *outs):
    for s in range(HEADS):
        both = mine_ref[s] + theirs_ref[s].astype(jnp.float32)
        outs[s][:BLOCK, :] = both.astype(jnp.bfloat16)
        outs[s][BLOCK:, :] = dq_ref[s]


def unpack_kernel(*rest):
    order = (0,) + ORDER_BACK
    parts = [rest[order.index(s)] for s in range(HEADS)]
    dq_out, dk_out, dv_out, dq_ref, dk_ref, dv_ref, messages, sems = rest[HEADS:]
    me = number()
    head_dim = LANES // 2
    for s in range(HEADS):
        messages[me ^ s] = parts[s][...]
    copies = [
        pltpu.make_async_copy(a, b, sems.at[n])
        for n, (a, b) in enumerate(((dk_ref, dk_out), (dv_ref, dv_out), (dq_ref, dq_out)))
    ]
    for target, first, copy in ((dk_ref, 0, copies[0]), (dv_ref, head_dim, copies[1])):
        for h in range(0, HEADS, 2):
            cols = slice(h * head_dim, (h + 2) * head_dim)
            pair = [messages[h + n, :BLOCK, first : first + head_dim] for n in range(2)]
            target[:, cols] = jnp.concatenate(pair, axis=1)
        copy.start()
    for h in range(0, HEADS, 2):
        cols = slice(h * head_dim, (h + 2) * head_dim)
        turned = jnp.concatenate([messages[h, BLOCK:, :], messages[h + 1, BLOCK:, :]], axis=0)
        dq_ref[:, cols] = turned.astype(jnp.float32).T.astype(jnp.bfloat16)
    copies[2].start()
    for copy in copies:
        copy.wait()


def exchange(parts, order):
    moved = {0: parts[0]}
    for s in order:
        pairs = [(j, j ^ s) for j in range(HEADS)]
        moved[s] = lax.ppermute(parts[s], ("across", "col"), pairs)
    return moved


def gather_keys(own, shares, share):
    if shares == 2:
        return lax.ppermute(own, "share", [(0, 1), (1, 0)])
    gathered = lax.all_gather(own, "share", axis=0, tiled=False)
    return gathered[jnp.arange(1, shares) ^ share].reshape(-1, LANES)


def sum_shares(theirs, shares, share):
    if shares == 2:
        return lax.ppermute(theirs, "share", [(0, 1), (1, 0)])
    full = jnp.zeros((shares, HEADS, BLOCK, LANES), jnp.float32)
    parts = theirs.reshape(shares - 1, HEADS, BLOCK, LANES).astype(jnp.float32)
    full = full.at[jnp.arange(1, shares) ^ share].set(parts)
    return lax.psum_scatter(full, "share", scatter_dimension=0, tiled=False)


def call(kernel, outs, in_specs, scratch=(), tiles=0, aliases=None, out_space=VMEM):
    flops = tiles * 10 * BLOCK * BLOCK * (LANES // 2)
    cost = pl.CostEstimate(flops=flops, bytes_accessed=tiles << 14, transcendentals=tiles * BLOCK * BLOCK)
    return pl.pallas_call(
        kernel,
        out_shape=[jax.ShapeDtypeStruct(shape, dtype) for shape, dtype in outs],
        in_specs=in_specs,
        out_specs=[out_space] * len(outs),
        scratch_shapes=list(scratch),
        cost_estimate=cost,
        input_output_aliases=aliases or {},
        compiler_params=pltpu.CompilerParams(vmem_limit_bytes=48 * 1024 * 1024),
    )


def body(queries, keys, values, outputs, out_grad, log_norm, contacts):
    bf16, f32 = jnp.bfloat16, jnp.float32
    width = queries.shape[1]
    columns = lax.axis_size("col")
    across = lax.axis_size("across")
    shares = lax.axis_size("share")
    contact_count = contacts.shape[1]
    sizes = (shares, across, columns, contact_count)
    count = shares * HEADS
    half = LANES // 2
    share = lax.axis_index("share")
    length = 2 * BLOCK + STATS
    loaded = [
        pltpu.with_memory_space_constraint(a, pltpu.HBM)
        for a in (contacts, queries, keys, values, outputs, out_grad, log_norm)
    ]
    packed = call(
        lambda *refs: pack_kernel(sizes, *refs),
        [((length, LANES), bf16)] * HEADS,
        [HBM] * 7,
        [
            pltpu.VMEM((HEADS, length, LANES), bf16),
            pltpu.SMEM(contacts.shape, jnp.int32),
            *[pltpu.VMEM(a.shape, a.dtype) for a in loaded[1:]],
            pltpu.SemaphoreType.DMA((7,)),
        ],
    )(*loaded)
    moved = exchange(packed, ORDER_OUT)
    early, late = [moved[s] for s in EARLY], [moved[s] for s in LATE]
    plan = contact_plan(sizes)
    held = [
        ((count, BLOCK, LANES), bf16),
        ((count, half, LANES), bf16),
        ((HEADS, 2 * BLOCK, LANES), bf16),
        ((count, BLOCK, LANES), f32),
        ((HEADS, half, BLOCK), f32),
    ]
    others = [
        gather_keys(jnp.concatenate([moved[s][:BLOCK] for s in slots], axis=0), shares, share) for slots in GROUPS
    ]
    kv, kt, weights, total, dq = call(
        lambda *refs: early_kernel(sizes, *refs),
        held,
        [VMEM] * (len(EARLY) + len(GROUPS)),
    )(*early, *others)
    own = call(late_kernel, [((len(LATE) * BLOCK, LANES), bf16)], [VMEM] * (len(LATE) + 1))(*late, dq)[0]
    other = gather_keys(own, shares, share)
    kv, kt, weights, total, dq = call(
        lambda *refs: first_kernel(sizes, *refs),
        held,
        [VMEM] * (HEADS + 5),
        tiles=HEADS * (plan[2] - plan[1]) + len(LATE) * plan[0],
        aliases={HEADS + n: n for n in range(5)},
    )(*early, *late, kv, kt, weights, total, dq)
    kv, kt, total, dq, theirs = call(
        lambda *refs: second_kernel(sizes, *refs),
        [held[0], held[1], held[3], held[4], ((count - HEADS, BLOCK, LANES), bf16)],
        [VMEM] * (HEADS + 6),
        tiles=HEADS * (plan[1] - plan[0]),
        aliases={HEADS + 1: 0, HEADS + 2: 1, HEADS + 4: 2, HEADS + 5: 3},
    )(*early, *late, other, kv, kt, weights, total, dq)
    arrived = sum_shares(theirs, shares, share)
    mine, dq = call(
        lambda *refs: third_kernel(sizes, *refs),
        [((HEADS, BLOCK, LANES), f32), ((HEADS, half, BLOCK), bf16)],
        [VMEM] * (HEADS + 5),
        [pltpu.VMEM((HEADS, BLOCK, LANES), f32)],
        tiles=HEADS * (plan[3] - plan[2]) + 1,
    )(*early, *late, kv, kt, weights, total, dq)
    joined = call(
        join_kernel,
        [((BLOCK + half, LANES), bf16)] * HEADS,
        [VMEM] * 3,
    )(mine, arrived, dq)
    back = exchange(joined, ORDER_BACK)
    return call(
        unpack_kernel,
        [((BLOCK, width), bf16)] * 3,
        [VMEM] * HEADS,
        [pltpu.VMEM((BLOCK, width), bf16)] * 3
        + [pltpu.VMEM((HEADS, BLOCK + half, LANES), bf16), pltpu.SemaphoreType.DMA((3,))],
        out_space=HBM,
    )(*[back[s] for s in (0,) + ORDER_BACK])


def solution(mesh):
    groups, rows, columns = (mesh.shape[a] for a in ("groups", "row", "col"))
    across = HEADS // columns
    shape = (groups, across, rows // across, columns)
    split = Mesh(mesh.devices.reshape(shape), ("groups", "across", "share", "col"))
    query_side = ("groups", "across", "share", "col")
    key_side = ("groups", "col", "across", "share")
    in_specs = (
        P(query_side, None),
        P(key_side, None),
        P(key_side, None),
        P(query_side, None),
        P(query_side, None),
        P(None, query_side),
        P(("groups", "across", "share"), None),
    )
    out_specs = (P(query_side, None), P(key_side, None), P(key_side, None))
    return jax.shard_map(body, mesh=split, in_specs=in_specs, out_specs=out_specs, check_vma=False)
```
